128 devices in a mesh: gx: 4 (over x), gy: 4 (over y), gz: 8 (over z, core).
Axes of the slice: x: 4, y: 4, z: 4, core: 2. Of those that a mesh axis runs over, the one named last changes fastest.
Arguments:
- right_side: float32 [32, 256, 1024], P('gx', 'gy', 'gz'), may hold values from -40 to 40
- phase: int32 [32, 256, 1024], P('gx', 'gy', 'gz'), may hold values from 0 to 1
- deflation_weights: float32 [32, 256, 1024], P('gx', 'gy', 'gz'), may hold values from -0.1875 to 0.1875
- coarse_inverse: float32 [8192, 8192], P(('gx', 'gy', 'gz')), may hold values from 0 to 16, as said below
Outputs:
- pressure: float32 [32, 256, 1024], P('gx', 'gy', 'gz')
- residual: float32 [32, 256, 1024], P('gx', 'gy', 'gz')
The draws below stay inside these ranges and needn't reach their ends.
Inputs may be any that keep to these rules, and one draw needn't show every extreme that they name: `coarse_inverse`: symmetric and positive definite, with nonnegative entries.
All inputs are finite; a program needn't handle non-finite values.
Results may differ from the reference program's by a relative error of at most 0.0003.
Values sent between devices are 32-bit elements; how exact they have to be, the bound alone decides.
No kernel may reach another device: no remote copies, remote signals or barrier semaphores. Data moves between devices by JAX's collectives and lax.ppermute only.
A program may use at most 64 MiB of HBM per device.

```python
import math
import jax
import jax.numpy as jnp
from jax import lax

CX = 8
CY = 64
CZ = 128
SBX = 4
SBY = 4
SBZ = 4
ND = 64
DEG = 6
ITERS = 2
NX = 32
NY = 256
NZ = 1024
K = 8192
BLOCKS_Y = 4
BLOCKS_Z = 8
N_GX = 4
N_GY = 4
N_GZ = 8


def draw_right_side(key, part):
    key = jax.random.fold_in(key, 7)
    along_x = (jnp.arange(NX, dtype=jnp.float32) + 0.5) / NX
    rough = jax.random.truncated_normal(key, -4.0, 4.0, (NX, NY, NZ), jnp.float32)
    rising = jnp.power(10.0, along_x)[:, None, None]
    return rough * rising


def draw_phase(key, part):
    key = jax.random.fold_in(key, 29)
    key_radius, key_x, key_y, key_z = jax.random.split(key, 4)
    side = CX // 2
    lattice = (NX // side, NY // side, NZ // side)
    low_radius = max(1, side // 4)
    high_radius = max(low_radius + 1, (side - 1) // 2 + 1)
    radius = jax.random.randint(key_radius, lattice, low_radius, high_radius, jnp.int32)
    centre_x = jax.random.randint(key_x, lattice, radius, side - radius, jnp.int32)
    centre_y = jax.random.randint(key_y, lattice, radius, side - radius, jnp.int32)
    centre_z = jax.random.randint(key_z, lattice, radius, side - radius, jnp.int32)
    cells_x = jnp.arange(NX, dtype=jnp.int32)
    cells_y = jnp.arange(NY, dtype=jnp.int32)
    cells_z = jnp.arange(NZ, dtype=jnp.int32)
    index_x = (cells_x // side)[:, None, None]
    index_y = (cells_y // side)[None, :, None]
    index_z = (cells_z // side)[None, None, :]
    offset_x = (cells_x % side)[:, None, None]
    offset_y = (cells_y % side)[None, :, None]
    offset_z = (cells_z % side)[None, None, :]
    own_radius = radius[index_x, index_y, index_z]
    delta_x = offset_x - centre_x[index_x, index_y, index_z]
    delta_y = offset_y - centre_y[index_x, index_y, index_z]
    delta_z = offset_z - centre_z[index_x, index_y, index_z]
    distance = delta_x * delta_x + delta_y * delta_y + delta_z * delta_z
    return jnp.where(distance <= own_radius * own_radius, 1, 0).astype(jnp.int32)


def draw_coarse_inverse(key, part):
    key = jax.random.fold_in(key, 13)
    first, second = jax.random.split(key)
    index = jnp.arange(K)
    block = index // ND
    inside = index % ND
    pos_x = block // (BLOCKS_Y * BLOCKS_Z) * SBX + inside // (SBY * SBZ)
    pos_y = block // BLOCKS_Z % BLOCKS_Y * SBY + inside // SBZ % SBY
    pos_z = block % BLOCKS_Z * SBZ + inside % SBZ
    delta_x = (pos_x[:, None] - pos_x[None, :]).astype(jnp.float32)
    delta_y = (pos_y[:, None] - pos_y[None, :]).astype(jnp.float32)
    delta_z = (pos_z[:, None] - pos_z[None, :]).astype(jnp.float32)
    distance = jnp.sqrt(delta_x * delta_x + delta_y * delta_y + delta_z * delta_z)
    reach = 1.0 * SBX
    kernel = jnp.exp(-distance / reach)
    normal_factor = 1.0 / (8.0 * math.pi * reach * reach * reach)
    lowest, highest = (0.5, 2.0)
    scales = jnp.exp(jax.random.uniform(first, (K,), jnp.float32, math.log(lowest), math.log(highest)))
    extra = jnp.exp(jax.random.uniform(second, (K,), jnp.float32, 0.0, math.log(4.0)))
    diagonal_part = jnp.where(index[:, None] == index[None, :], extra[:, None], 0.0)
    return scales[:, None] * scales[None, :] * (kernel + diagonal_part) * normal_factor


def level_of(key, shape, cuts, low, largest):
    loudness, own = 1.0, jax.random.fold_in(key, 6)
    for axis_at, shards_of in cuts:
        heights = jnp.exp(jax.random.uniform(jax.random.fold_in(own, axis_at), (shards_of,), jnp.float32, low / len(cuts), largest / len(cuts)))
        loudness = loudness * jnp.repeat(heights, shape[axis_at] // shards_of).reshape([-1 if axis == axis_at else 1 for axis in range(len(shape))])
    return loudness


def normal_values(own_key, extent, width, bound, shards=(), held_as=jnp.bfloat16):
    values = width * jax.random.normal(own_key, extent, jnp.float32)
    if shards:
        values = values * level_of(own_key, extent, shards, -0.22, 0.18)
    return jnp.clip(values, -bound, bound).astype(held_as)


def setup_inputs(seed: int = 0) -> dict:
    splits = jax.random.split(jax.random.key(seed), 5)
    right_side = draw_right_side(jax.random.fold_in(splits[4], 71), 0)
    phase = draw_phase(jax.random.fold_in(splits[4], 71), 0)
    deflation_weights = normal_values(splits[2], (NX, NY, NZ), (CX * CY * CZ // ND) ** -0.5, 0.1875, ((0, 4), (1, 4), (2, 8)), jnp.float32)
    coarse_inverse = draw_coarse_inverse(jax.random.fold_in(splits[4], 71), 0)
    return dict(right_side=right_side, phase=phase, deflation_weights=deflation_weights, coarse_inverse=coarse_inverse)


spectrum_low = 0.08
spectrum_high = 2.0


def recurrence():
    center = 0.5 * (spectrum_high + spectrum_low)
    half_width = 0.5 * (spectrum_high - spectrum_low)
    ratio = center / half_width
    earlier = 1.0 / ratio
    weights = []
    for index in range(DEG - 1):
        later = 1.0 / (2.0 * ratio - earlier)
        weights.append((later * earlier, 2.0 * later / half_width))
        earlier = later
    return 1.0 / center, weights


def coefficients(density_pad):
    face_x = 2.0 / (density_pad[1:, 1:-1, 1:-1] + density_pad[:-1, 1:-1, 1:-1])
    face_y = 2.0 / (density_pad[1:-1, 1:, 1:-1] + density_pad[1:-1, :-1, 1:-1])
    face_z = 2.0 / (density_pad[1:-1, 1:-1, 1:] + density_pad[1:-1, 1:-1, :-1])
    diagonal = face_x[:-1] + face_x[1:] + face_y[:, :-1] + face_y[:, 1:] + face_z[:, :, :-1] + face_z[:, :, 1:]
    return (face_x, face_y, face_z), diagonal


def stencil(padded, faces):
    flux_x = faces[0] * (padded[1:, 1:-1, 1:-1] - padded[:-1, 1:-1, 1:-1])
    flux_y = faces[1] * (padded[1:-1, 1:, 1:-1] - padded[1:-1, :-1, 1:-1])
    flux_z = faces[2] * (padded[1:-1, 1:-1, 1:] - padded[1:-1, 1:-1, :-1])
    return (flux_x[:-1] - flux_x[1:]) + (flux_y[:, :-1] - flux_y[:, 1:]) + (flux_z[:, :, :-1] - flux_z[:, :, 1:])


def smooth(residual, faces, diagonal):
    first_scale, weights = recurrence()
    step = (residual / diagonal) * first_scale
    result = step
    for keep, push in weights:
        image = stencil(jnp.pad(result, 1), faces)
        step = keep * step + push * ((residual - image) / diagonal)
        result = result + step
    return result


def deflate(residual, deflation_weights, coarse_inverse):
    layout = (N_GX * SBX, CX // SBX, N_GY * SBY, CY // SBY, N_GZ * SBZ, CZ // SBZ)
    totals = (deflation_weights * residual).reshape(layout).sum(axis=(1, 3, 5))
    ordered = totals.reshape(N_GX, SBX, N_GY, SBY, N_GZ, SBZ).transpose(0, 2, 4, 1, 3, 5).reshape(K)
    amounts = jnp.dot(coarse_inverse, ordered, precision=lax.Precision.HIGHEST)
    placed = amounts.reshape(N_GX, N_GY, N_GZ, SBX, SBY, SBZ).transpose(0, 3, 1, 4, 2, 5)
    placed = placed.reshape(N_GX * SBX, 1, N_GY * SBY, 1, N_GZ * SBZ, 1)
    return (deflation_weights.reshape(layout) * placed).reshape(NX, NY, NZ)


def reference(right_side, phase, deflation_weights, coarse_inverse):
    density = jnp.where(phase == 1, 0.001, 1.0).astype(jnp.float32)
    faces, diagonal = coefficients(jnp.pad(density, 1, constant_values=1.0))

    def precondition(field):
        return smooth(field, faces, diagonal) + deflate(field, deflation_weights, coarse_inverse)

    pressure = jnp.zeros_like(right_side)
    residual = right_side
    precond = precondition(residual)
    energy = jnp.sum(residual * precond)
    direction = precond
    for index in range(ITERS):
        image = stencil(jnp.pad(direction, 1), faces)
        step_size = energy / jnp.sum(direction * image)
        pressure = pressure + step_size * direction
        residual = residual - step_size * image
        if index + 1 < ITERS:
            precond = precondition(residual)
            energy_next = jnp.sum(residual * precond)
            direction = precond + (energy_next / energy) * direction
            energy = energy_next
    return pressure, residual
```

```python
import functools

import jax
import jax.numpy as jnp
import numpy as np
from jax import lax
from jax.experimental import pallas as pl
from jax.experimental.pallas import tpu as pltpu
from jax.sharding import PartitionSpec as P

AXES = ("gx", "gy", "gz")
SBX = 4
ND = 64
DEG = 6
spectrum_low = 0.08
spectrum_high = 2.0

CX, CY, CZ = 8, 64, 128
HX, HY = 7, 8
PX, PY, PZ = CX + 2 * HX, CY + 2 * HY, 2 * CZ
H_R, H_G, H_V = 5, 7, 1
N_R, N_G, N_V = CX + 2 * H_R, CX + 2 * H_G, CX + 2 * H_V
N_ALL = N_R + N_G + N_V
GROUPS = -(-N_ALL // 16)
GROUPS_P = -(-PX // 16)
NDEV = 128

LIQUID = np.float32(1.0)
GAS = np.float32(0.001)
F_LL = np.float32(2.0) / (LIQUID + LIQUID)
F_LG = np.float32(2.0) / (LIQUID + GAS)
F_GG = np.float32(2.0) / (GAS + GAS)

F32 = jnp.float32
EXACT = lax.Precision.HIGHEST


def recurrence():
    center = 0.5 * (spectrum_high + spectrum_low)
    half_width = 0.5 * (spectrum_high - spectrum_low)
    ratio = center / half_width
    earlier = 1.0 / ratio
    weights = []
    for index in range(DEG - 1):
        later = 1.0 / (2.0 * ratio - earlier)
        weights.append((later * earlier, 2.0 * later / half_width))
        earlier = later
    return (1.0 / center, weights)


def iota(shape, dim):
    return lax.broadcasted_iota(jnp.int32, shape, dim)


def neighbours(ref, i):
    v = ref[i]
    return (
        ref[i - 1],
        ref[i + 1],
        pltpu.roll(v, 1, 0),
        pltpu.roll(v, PY - 1, 0),
        pltpu.roll(v, 1, 1),
        pltpu.roll(v, PZ - 1, 1),
    )


def inside_yz(pos):
    gy, gz = pos[1], pos[2]
    row = iota((PY, PZ), 0) - HY + gy * CY
    lane = iota((PY, PZ), 1)
    near = jnp.where(lane < CZ + CZ // 2, lane, lane - PZ) + gz * CZ
    kept = (lane < CZ + 8) | (lane >= PZ - 8)
    good = (row >= 0) & (row < 4 * CY) & (near >= 0) & (near < 8 * CZ) & kept
    return jnp.where(good, 1.0, 0.0).astype(F32)


def inside_x(pos, rel):
    x = pos[0] * CX + rel
    return jnp.where((x >= 0) & (x < 4 * CX), 1.0, 0.0).astype(F32)


def pair(labels):
    gas = labels > 0.5
    return jnp.where(gas, F_LG, F_LL), jnp.where(gas, F_GG - F_LG, F_LG - F_LL)


def row_sums(parts):
    rows = []
    for part in parts:
        for sy in range(4):
            rows.append(jnp.sum(part[16 * sy : 16 * sy + 16], axis=0, keepdims=True))
    stacked = jnp.concatenate(rows, axis=0)
    pick = jnp.where(iota((128, 128), 0) // 32 == iota((128, 128), 1) % 4, 1.0, 0.0).astype(F32)
    spread = jnp.dot(stacked, pick, precision=EXACT, preferred_element_type=F32)
    keep = (iota((16, 128), 1) // 4) % 16 == iota((16, 128), 0)
    return jnp.sum(jnp.where(keep, spread, 0.0), axis=0, keepdims=True)


def fields(rows):
    count = len(rows)
    keep = (iota((16, 128), 1) // 4 == iota((16, 128), 0)) & (iota((16, 128), 1) < ND)
    tall = jnp.concatenate([jnp.where(keep, jnp.broadcast_to(r, (16, 128)), 0.0) for r in rows], axis=0)
    pick = jnp.where(iota((128, 128), 0) % 4 == iota((128, 128), 1) // 32, 1.0, 0.0).astype(F32)
    out = jnp.dot(tall, pick, precision=EXACT, preferred_element_type=F32)
    return [out[16 * k : 16 * k + 16] for k in range(count)]


def plane_field(field, sx):
    return jnp.concatenate(
        [jnp.broadcast_to(field[4 * sx + sy : 4 * sx + sy + 1], (16, 128)) for sy in range(4)], axis=0
    )


def coarse_rows(matrix_ref, even, odd):
    wide = jnp.where(iota((64, 128), 1) < ND, even, odd)
    total = matrix_ref[:, 0:128] * wide[0:1]
    for t in range(1, 64):
        total = total + matrix_ref[:, 128 * t : 128 * t + 128] * wide[t : t + 1]
    column = jnp.sum(total, axis=1, keepdims=True)
    keep = iota((64, 128), 1) % ND == iota((64, 128), 0)
    return jnp.sum(jnp.where(keep, column, 0.0), axis=0, keepdims=True)


def total_sum(x):
    return jnp.sum(jnp.sum(x, axis=0, keepdims=True), axis=1, keepdims=True)


def start_kernel(r_ref, phase_ref, v_ref, xl_ref, xr_ref, send_ref):
    parts = []
    for sx in range(4):
        parts.append(r_ref[2 * sx] * v_ref[2 * sx] + r_ref[2 * sx + 1] * v_ref[2 * sx + 1])
    send_ref[...] = jnp.broadcast_to(row_sums(parts), (NDEV, 128))
    xl_ref[0:H_R] = r_ref[0:H_R]
    xr_ref[0:H_R] = r_ref[CX - H_R :]
    xl_ref[H_R : H_R + H_G] = jnp.where(phase_ref[0:H_G] == 1, 1.0, 0.0).astype(F32)
    xr_ref[H_R : H_R + H_G] = jnp.where(phase_ref[CX - H_G :] == 1, 1.0, 0.0).astype(F32)
    xl_ref[H_R + H_G :] = v_ref[0:H_V]
    xr_ref[H_R + H_G :] = v_ref[CX - H_V :]


def stacked_planes(r_ref, phase_ref, v_ref, fl_ref, fr_ref):
    planes = []
    for halo, own, base in ((H_R, "r", 0), (H_G, "g", H_R), (H_V, "v", H_R + H_G)):
        for rel in range(-halo, CX + halo):
            if rel < 0:
                planes.append(lambda s, k=base + rel + halo: fl_ref[k, s])
            elif rel >= CX:
                planes.append(lambda s, k=base + rel - CX: fr_ref[k, s])
            elif own == "r":
                planes.append(lambda s, k=rel: r_ref[k, s])
            elif own == "g":
                planes.append(lambda s, k=rel: jnp.where(phase_ref[k, s] == 1, 1.0, 0.0).astype(F32))
            else:
                planes.append(lambda s, k=rel: v_ref[k, s])
    return planes


def y_kernel(r_ref, phase_ref, v_ref, fl_ref, fr_ref, yl_ref, yr_ref):
    planes = stacked_planes(r_ref, phase_ref, v_ref, fl_ref, fr_ref)
    for k, plane in enumerate(planes):
        yl_ref[k] = plane(pl.ds(0, HY))
        yr_ref[k] = plane(pl.ds(CY - HY, HY))


def pack_lanes(ext_ref, zl_ref, zr_ref, count):
    slot = iota((PY, CZ), 1) // 8
    for group in range(zl_ref.shape[0]):
        left = jnp.zeros((PY, CZ), F32)
        right = jnp.zeros((PY, CZ), F32)
        for m in range(16):
            k = 16 * group + m
            if k >= count:
                break
            plane = ext_ref[k]
            left = jnp.where(slot == m, pltpu.roll(plane, 8 * m, 1) if m else plane, left)
            shift = (8 * m + 8) % CZ
            right = jnp.where(slot == m, pltpu.roll(plane, shift, 1) if shift else plane, right)
        zl_ref[group] = left
        zr_ref[group] = right


def wide_plane(ext_ref, fl_ref, fr_ref, k):
    group, m = k // 16, k % 16
    lane = iota((PY, CZ), 1)
    shift = (CZ - 8 * m) % CZ
    ahead = pltpu.roll(fr_ref[group], shift, 1) if shift else fr_ref[group]
    shift = (CZ - 8 - 8 * m) % CZ
    behind = pltpu.roll(fl_ref[group], shift, 1) if shift else fl_ref[group]
    side = jnp.where(lane < 8, ahead, jnp.where(lane >= CZ - 8, behind, 0.0))
    return jnp.concatenate([ext_ref[k], side], axis=1)


def z_kernel(r_ref, phase_ref, v_ref, fl_ref, fr_ref, yd_ref, yu_ref, ext_ref, zl_ref, zr_ref):
    planes = stacked_planes(r_ref, phase_ref, v_ref, fl_ref, fr_ref)
    for k, plane in enumerate(planes):
        ext_ref[k, 0:HY] = yd_ref[k]
        ext_ref[k, HY : HY + CY] = plane(pl.ds(0, CY))
        ext_ref[k, HY + CY :] = yu_ref[k]
    pack_lanes(ext_ref, zl_ref, zr_ref, N_ALL)


def y2_kernel(p_ref, fl_ref, fr_ref, yl_ref, yr_ref):
    for i in range(PX):
        rel = i - HX
        src, k = (fl_ref, i) if rel < 0 else (fr_ref, rel - CX) if rel >= CX else (p_ref, rel)
        yl_ref[i] = src[k, 0:HY]
        yr_ref[i] = src[k, CY - HY :]


def z2_kernel(p_ref, fl_ref, fr_ref, yd_ref, yu_ref, ext_ref, zl_ref, zr_ref):
    for i in range(PX):
        rel = i - HX
        src, k = (fl_ref, i) if rel < 0 else (fr_ref, rel - CX) if rel >= CX else (p_ref, rel)
        ext_ref[i, 0:HY] = yd_ref[i]
        ext_ref[i, HY : HY + CY] = src[k]
        ext_ref[i, HY + CY :] = yu_ref[i]
    pack_lanes(ext_ref, zl_ref, zr_ref, PX)


def chebyshev(halo, w_ref, rp_ref, a_ref, b_ref):
    _, weights = recurrence()
    now, before = a_ref, b_ref
    for index, (keep, push) in enumerate(weights):
        halo -= 1

        def body(i, carry, now=now, before=before, first=index == 0, keep=keep, push=push):
            around = neighbours(now, i)
            total = rp_ref[i]
            for d in range(6):
                total = total + w_ref[d, i] * around[d]
            new = (1.0 + keep - push) * now[i] + push * total
            if not first:
                new = new - keep * before[i]
            before[i] = new
            return carry

        lax.fori_loop(HX - halo, HX + CX + halo, body, 0)
        now, before = before, now
    return now


def smooth_kernel(pos, ext_ref, zl_ref, zr_ref, sums_ref, matrix_ref, p_ref, xl_ref, xr_ref, g_ref, v_ref, w_ref, rp_ref, a_ref, b_ref):
    mask = inside_yz(pos)
    for i in range(PX):
        g_ref[i] = wide_plane(ext_ref, zl_ref, zr_ref, N_R + i) * (mask * inside_x(pos, i - HX))
    for i in range(N_V):
        v_ref[i] = wide_plane(ext_ref, zl_ref, zr_ref, N_R + N_G + i) * (mask * inside_x(pos, i - H_V))
    for k in range(N_R):
        rp_ref[k - H_R + HX] = wide_plane(ext_ref, zl_ref, zr_ref, k)
    first_scale, _ = recurrence()

    def prepare(i, carry):
        around = neighbours(g_ref, i)
        first, second = pair(g_ref[i])
        count = (around[0] + around[1]) + (around[2] + around[3]) + (around[4] + around[5])
        inverse = inside_yz(pos) * inside_x(pos, i - HX) / (6.0 * first + second * count)
        first, second = first * inverse, second * inverse
        for d in range(6):
            w_ref[d, i] = first + second * around[d]
        scaled = rp_ref[i] * inverse
        rp_ref[i] = scaled
        a_ref[i] = scaled * first_scale
        return carry

    lax.fori_loop(HX - H_R, HX + CX + H_R, prepare, 0)
    result = chebyshev(H_R, w_ref, rp_ref, a_ref, b_ref)
    even = sums_ref[pl.ds(0, 64, stride=2), :]
    odd = sums_ref[pl.ds(1, 64, stride=2), :]
    amounts = coarse_rows(matrix_ref, even, odd)
    (field,) = fields([amounts])
    for x in range(CX):
        value = result[HX + x, HY : HY + CY, 0:CZ]
        value = value + v_ref[x + H_V, HY : HY + CY, 0:CZ] * plane_field(field, x // 2)
        p_ref[x] = value
        if x < HX:
            xl_ref[x] = value
        if x >= CX - HX:
            xr_ref[x - CX + HX] = value


def product_kernel(g_ref, v_ref, out_ref):
    last_y = iota((CY, CZ), 0) % 16 == 15
    last_z = iota((CY, CZ), 1) % 32 == 31
    quads = [[], [], [], []]

    def own(a):
        return a[HY : HY + CY, 0:CZ]

    for sx in range(4):
        sums = [jnp.zeros((CY, CZ), F32) for _ in range(4)]
        for x in (2 * sx, 2 * sx + 1):
            labels = neighbours(g_ref, x + HX)
            values = neighbours(v_ref, x + H_V)
            first, second = pair(own(g_ref[x + HX]))
            mine = own(v_ref[x + H_V])
            count = sum(own(a) for a in labels)
            sums[0] = sums[0] + (6.0 * first + second * count) * mine * mine
            cross = [(first + second * own(labels[d])) * mine * own(values[d]) for d in (1, 3, 5)]
            if x % 2 == 0:
                sums[0] = sums[0] - 2.0 * cross[0]
            else:
                sums[1] = sums[1] - cross[0]
            sums[0] = sums[0] - 2.0 * jnp.where(last_y, 0.0, cross[1]) - 2.0 * jnp.where(last_z, 0.0, cross[2])
            sums[2] = sums[2] - jnp.where(last_y, cross[1], 0.0)
            sums[3] = sums[3] - jnp.where(last_z, cross[2], 0.0)
        for n in range(4):
            quads[n].append(sums[n])
    for n in range(4):
        out_ref[n : n + 1] = row_sums(quads[n])


def image_plane(ref, i, first, second, labels):
    mine = ref[i]
    around = neighbours(ref, i)
    total = (first + second * labels[0]) * (mine - around[0])
    for d in range(1, 6):
        total = total + (first + second * labels[d]) * (mine - around[d])
    return total


def image_kernel(
    pos, ext_ref, zl_ref, zr_ref, g_ref, r_ref, v_ref, e_ref, q_ref, c_ref, y_ref, send_ref, full_ref, w_ref, rp_ref, a_ref, b_ref
):
    mask = inside_yz(pos)
    for i in range(PX):
        full_ref[i] = wide_plane(ext_ref, zl_ref, zr_ref, i) * (mask * inside_x(pos, i - HX))
    first_scale, _ = recurrence()

    def prepare(i, carry):
        labels = neighbours(g_ref, i)
        first, second = pair(g_ref[i])
        count = (labels[0] + labels[1]) + (labels[2] + labels[3]) + (labels[4] + labels[5])
        inverse = inside_yz(pos) * inside_x(pos, i - HX) / (6.0 * first + second * count)
        image = image_plane(full_ref, i, first, second, labels)
        b_ref[i] = image
        first, second = first * inverse, second * inverse
        for d in range(6):
            w_ref[d, i] = first + second * labels[d]
        scaled = image * inverse
        rp_ref[i] = scaled
        a_ref[i] = scaled * first_scale
        return carry

    lax.fori_loop(1, PX - 1, prepare, 0)
    parts = []
    energy = jnp.zeros((CY, CZ), F32)
    curve = jnp.zeros((CY, CZ), F32)
    for x in range(CX):
        image = b_ref[HX + x, HY : HY + CY, 0:CZ]
        value = full_ref[HX + x, HY : HY + CY, 0:CZ]
        q_ref[x] = image
        energy = energy + r_ref[x] * value
        curve = curve + image * value
        term = v_ref[x] * image
        if x % 2 == 0:
            parts.append(term)
        else:
            parts[-1] = parts[-1] + term
    result = chebyshev(HX - 1, w_ref, rp_ref, a_ref, b_ref)
    for x in range(CX):
        i = HX + x
        first, second = pair(g_ref[i])
        image = image_plane(result, i, first, second, neighbours(g_ref, i))
        c_ref[x] = result[i, HY : HY + CY, 0:CZ]
        y_ref[x] = image[HY : HY + CY, 0:CZ]
    lane = iota((1, 128), 1)
    scalars = jnp.where(lane == 64, total_sum(energy), jnp.where(lane == 65, total_sum(curve), 0.0))
    send = jnp.concatenate(
        [
            jnp.where(lane < ND, row_sums(parts), e_ref[0:1]),
            jnp.where(lane < ND, e_ref[1:2], e_ref[2:3]),
            jnp.where(lane < ND, e_ref[3:4], scalars),
        ],
        axis=1,
    )
    send_ref[...] = jnp.broadcast_to(send, (NDEV, 384))


def first_scalars(sums_ref):
    totals = jnp.sum(sums_ref[:, 256:384], axis=0, keepdims=True)
    energy = totals[0:1, 64:65]
    curve = totals[0:1, 65:66]
    return energy, curve, energy / curve


def amounts_kernel(sums_ref, matrix_ref, p_ref, q_ref, c_ref, y_ref, v_ref, r_ref, send_ref, piece_ref):
    _, _, alpha = first_scalars(sums_ref)
    piece_ref[...] = sums_ref[:, 0:128]
    even = piece_ref[pl.ds(0, 64, stride=2), :]
    odd = pltpu.roll(piece_ref[pl.ds(1, 64, stride=2), :], 64, 1)
    amounts = coarse_rows(matrix_ref, even, odd)
    (field,) = fields([amounts])
    sums = [jnp.zeros((CY, CZ), F32) for _ in range(3)]
    for x in range(CX):
        lifted = v_ref[x] * plane_field(field, x // 2)
        p, q, c = p_ref[x], q_ref[x], c_ref[x]
        residual = r_ref[x] - alpha * q
        smooth = p - alpha * c
        smooth_image = q - alpha * y_ref[x]
        precond = smooth - alpha * lifted
        sums[0] = sums[0] + residual * precond
        sums[1] = sums[1] + precond * q
        sums[2] = sums[2] + smooth_image * (smooth - 2.0 * alpha * lifted)
    lane = iota((1, 128), 1)
    row = jnp.where(lane < ND, amounts, 0.0)
    for n in range(3):
        row = jnp.where(lane == ND + n, total_sum(sums[n]), row)
    send_ref[...] = jnp.broadcast_to(row, (NDEV, 128))


def final_kernel(
    pos, sums_ref, got_ref, p_ref, q_ref, c_ref, y_ref, r_ref, vx_ref, g_ref, pressure_ref, residual_ref, lift_ref
):
    energy, curve, alpha = first_scalars(sums_ref)
    got = got_ref[...]
    lane = iota((NDEV, 128), 1)
    dup = jnp.where(lane < ND, got, pltpu.roll(got, 64, 1))
    sz, sy, sx = lane % 4, (lane // 4) % 4, (lane // 16) % 4
    next_z = jnp.where(sz < 3, pltpu.roll(dup, 127, 1), pltpu.roll(pltpu.roll(dup, 3, 1), NDEV - 1, 0))
    next_y = jnp.where(sy < 3, pltpu.roll(dup, 124, 1), pltpu.roll(pltpu.roll(dup, 12, 1), NDEV - 8, 0))
    next_x = jnp.where(sx < 3, pltpu.roll(dup, 112, 1), pltpu.roll(pltpu.roll(dup, 48, 1), NDEV - 32, 0))
    one, two = sums_ref[:, 0:128], sums_ref[:, 128:256]
    three = sums_ref[:, 256:384]
    half = dup * pltpu.roll(one, 64, 1) + 2.0 * (next_x * two + next_y * pltpu.roll(two, 64, 1) + next_z * three)
    quad = total_sum(jnp.where(lane < ND, half * dup, 0.0))
    totals = jnp.sum(got, axis=0, keepdims=True)
    energy_next = totals[0:1, 64:65]
    mixed = totals[0:1, 65:66]
    beta = energy_next / energy
    curve_next = totals[0:1, 66:67] + alpha * alpha * quad + 2.0 * beta * mixed + beta * beta * curve
    alpha_next = energy_next / curve_next

    me = (pos[0] * 4 + pos[1]) * 8 + pos[2]
    rows = []
    for shift in (0, -32, 32, -8, 8, -1, 1):
        at = jnp.clip(me + shift, 0, NDEV - 1)
        rows.append(got_ref[pl.ds(at, 1), :])
    mine, xm, xp, ym, yp, zm, zp = fields(rows)
    lanes = iota((PY, CZ), 1)
    for i in range(N_V):
        x = i - H_V
        if x < 0 or x >= CX:
            own = plane_field(xm, 3) if x < 0 else plane_field(xp, 0)
            lift_ref[i, 0:HY] = jnp.zeros((HY, PZ), F32)
            lift_ref[i, HY + CY :] = jnp.zeros((HY, PZ), F32)
            lift_ref[i, HY : HY + CY, 0:CZ] = vx_ref[i, HY : HY + CY, 0:CZ] * own
            lift_ref[i, HY : HY + CY, CZ:PZ] = jnp.zeros((CY, CZ), F32)
            continue
        s = x // 2
        down = jnp.broadcast_to(ym[4 * s + 3 : 4 * s + 4], (HY, CZ))
        up = jnp.broadcast_to(yp[4 * s : 4 * s + 1], (HY, CZ))
        lift_ref[i, :, 0:CZ] = vx_ref[i, :, 0:CZ] * jnp.concatenate([down, plane_field(mine, s), up], axis=0)
        zeros = jnp.zeros((HY, CZ), F32)
        ahead = jnp.concatenate([zeros, plane_field(zp, s), zeros], axis=0)
        behind = jnp.concatenate([zeros, plane_field(zm, s), zeros], axis=0)
        side = jnp.where(lanes < 8, ahead, jnp.where(lanes >= CZ - 8, behind, 0.0))
        lift_ref[i, :, CZ:PZ] = vx_ref[i, :, CZ:PZ] * side
    for x in range(CX):
        first, second = pair(g_ref[x + HX])
        lifted_image = image_plane(lift_ref, x + H_V, first, second, neighbours(g_ref, x + HX))
        lifted_image = lifted_image[HY : HY + CY, 0:CZ]
        lifted = lift_ref[x + H_V, HY : HY + CY, 0:CZ]
        p, q = p_ref[x], q_ref[x]
        precond = p - alpha * (c_ref[x] + lifted)
        precond_image = q - alpha * (y_ref[x] + lifted_image)
        direction = precond + beta * p
        image = precond_image + beta * q
        pressure_ref[x] = alpha * p + alpha_next * direction
        residual_ref[x] = (r_ref[x] - alpha * q) - alpha_next * image


VMEM = pl.BlockSpec(memory_space=pltpu.VMEM)
SMEM = pl.BlockSpec(memory_space=pltpu.SMEM)


def call(kernel, outs, scratch=(), smem=False, cost=None):
    def run(*args):
        many = isinstance(outs, list)
        specs = [VMEM] * len(args)
        if smem:
            specs[0] = SMEM
        return pl.pallas_call(
            kernel,
            out_shape=[jax.ShapeDtypeStruct(s, F32) for s in outs] if many else jax.ShapeDtypeStruct(outs, F32),
            in_specs=specs,
            out_specs=[VMEM] * len(outs) if many else VMEM,
            scratch_shapes=[pltpu.VMEM(s, F32) for s in scratch],
            compiler_params=pltpu.CompilerParams(vmem_limit_bytes=48 * 1024 * 1024),
            cost_estimate=cost,
        )(*args)

    return run


def swap(to_left, to_right, axis):
    count = lax.axis_size(axis)
    from_right = lax.ppermute(to_left, axis, [((i + 1) % count, i) for i in range(count)])
    from_left = lax.ppermute(to_right, axis, [(i, (i + 1) % count) for i in range(count)])
    return from_left, from_right


def gather(rows):
    return lax.all_to_all(rows, AXES, 0, 0, tiled=True)


def local(right_side, phase, deflation_weights, coarse_inverse):
    pos = jnp.stack([lax.axis_index(a) for a in AXES]).astype(jnp.int32)
    block = (CX, CY, CZ)
    tall = (PX, PY, PZ)
    r, v = right_side, deflation_weights
    n_x = H_R + H_G + H_V
    xl, xr, send = call(start_kernel, [(n_x, CY, CZ), (n_x, CY, CZ), (NDEV, 128)])(r, phase, v)
    fl, fr = swap(xl, xr, "gx")
    sums = gather(send)
    yl, yr = call(y_kernel, [(N_ALL, HY, CZ)] * 2)(r, phase, v, fl, fr)
    yd, yu = swap(yl, yr, "gy")
    ext, zl, zr = call(z_kernel, [(N_ALL, PY, CZ), (GROUPS, PY, CZ), (GROUPS, PY, CZ)])(r, phase, v, fl, fr, yd, yu)
    zfl, zfr = swap(zl, zr, "gz")
    p, xl, xr, labels, v_wide = call(
        smooth_kernel,
        [block, (HX, CY, CZ), (HX, CY, CZ), tall, (N_V, PY, PZ)],
        scratch=[(6, *tall), tall, tall, tall],
        smem=True,
    )(pos, ext, zfl, zfr, sums, coarse_inverse)
    fl, fr = swap(xl, xr, "gx")
    quads = call(product_kernel, (4, 128), cost=pl.CostEstimate(flops=8_000_000, bytes_accessed=3_000_000, transcendentals=0))(
        labels, v_wide
    )
    yl, yr = call(y2_kernel, [(PX, HY, CZ)] * 2)(p, fl, fr)
    yd, yu = swap(yl, yr, "gy")
    ext, zl, zr = call(z2_kernel, [(PX, PY, CZ), (GROUPS_P, PY, CZ), (GROUPS_P, PY, CZ)])(p, fl, fr, yd, yu)
    zfl, zfr = swap(zl, zr, "gz")
    q, c, y, send = call(
        image_kernel,
        [block, block, block, (NDEV, 384)],
        scratch=[tall, (6, *tall), tall, tall, tall],
        smem=True,
    )(pos, ext, zfl, zfr, labels, r, v, quads)
    sums = gather(send)
    send = call(amounts_kernel, (NDEV, 128), scratch=[(NDEV, 128)])(sums, coarse_inverse, p, q, c, y, v, r)
    got = gather(send)
    pressure, residual = call(final_kernel, [block, block], scratch=[(N_V, PY, PZ)], smem=True)(
        pos, sums, got, p, q, c, y, r, v_wide, labels
    )
    return (pressure, residual)


def solution(mesh):
    return jax.shard_map(
        local,
        mesh=mesh,
        in_specs=(P(*AXES), P(*AXES), P(*AXES), P(AXES, None)),
        out_specs=(P(*AXES), P(*AXES)),
        check_vma=False,
    )
```

```python
import functools

import jax
import jax.numpy as jnp
import numpy as np
from jax import lax
from jax.experimental import pallas as pl
from jax.experimental.pallas import tpu as pltpu
from jax.sharding import PartitionSpec as P

AXES = ("gx", "gy", "gz")
SBX = 4
ND = 64
DEG = 6
spectrum_low = 0.08
spectrum_high = 2.0

CX, CY, CZ = 8, 64, 128
HX, HY = 7, 8
PX, PY, PZ = CX + 2 * HX, CY + 2 * HY, 2 * CZ
H_R, H_G, H_V = 5, 7, 1
N_R, N_G, N_V = CX + 2 * H_R, CX + 2 * H_G, CX + 2 * H_V
N_ALL = N_R + N_G + N_V
GROUPS = -(-N_ALL // 16)
GROUPS_P = -(-PX // 16)
NDEV = 128
ROWS = PY // 8

LIQUID = np.float32(1.0)
GAS = np.float32(0.001)
F_LL = np.float32(2.0) / (LIQUID + LIQUID)
F_LG = np.float32(2.0) / (LIQUID + GAS)
F_GG = np.float32(2.0) / (GAS + GAS)

F32 = jnp.float32
EXACT = lax.Precision.HIGHEST


def recurrence():
    center = 0.5 * (spectrum_high + spectrum_low)
    half_width = 0.5 * (spectrum_high - spectrum_low)
    ratio = center / half_width
    earlier = 1.0 / ratio
    weights = []
    for index in range(DEG - 1):
        later = 1.0 / (2.0 * ratio - earlier)
        weights.append((later * earlier, 2.0 * later / half_width))
        earlier = later
    return (1.0 / center, weights)


def iota(shape, dim):
    return lax.broadcasted_iota(jnp.int32, shape, dim)


def whole(ref, i):
    return jnp.concatenate([ref[0, i], ref[1, i]], axis=1)


def put(ref, i, plane):
    ref[0, i] = plane[:, 0:CZ]
    ref[1, i] = plane[:, CZ:PZ]


def neighbours(ref, i):
    v = whole(ref, i)
    return (
        whole(ref, i - 1),
        whole(ref, i + 1),
        pltpu.roll(v, 1, 0),
        pltpu.roll(v, PY - 1, 0),
        pltpu.roll(v, 1, 1),
        pltpu.roll(v, PZ - 1, 1),
    )


def strided(ref, i, j):
    rows = pl.ds(j, 8, stride=ROWS)
    return jnp.concatenate([ref[0, i, rows, :], ref[1, i, rows, :]], axis=1)


def around_strided(load, i, j):
    v = load(i, j)
    return (
        load(i - 1, j),
        load(i + 1, j),
        load(i, j - 1) if j else pltpu.roll(load(i, ROWS - 1), 1, 0),
        load(i, j + 1) if j < ROWS - 1 else pltpu.roll(load(i, 0), 7, 0),
        pltpu.roll(v, 1, 1),
        pltpu.roll(v, PZ - 1, 1),
    )


def inside_yz(pos, j=None):
    gy, gz = pos[1], pos[2]
    shape = (PY, PZ) if j is None else (8, PZ)
    row = iota(shape, 0) if j is None else iota(shape, 0) * ROWS + j
    row = row - HY + gy * CY
    lane = iota(shape, 1)
    near = jnp.where(lane < CZ + CZ // 2, lane, lane - PZ) + gz * CZ
    kept = (lane < CZ + 8) | (lane >= PZ - 8)
    good = (row >= 0) & (row < 4 * CY) & (near >= 0) & (near < 8 * CZ) & kept
    return jnp.where(good, 1.0, 0.0).astype(F32)


def inside_x(pos, rel):
    x = pos[0] * CX + rel
    return jnp.where((x >= 0) & (x < 4 * CX), 1.0, 0.0).astype(F32)


def pair(labels):
    gas = labels > 0.5
    return jnp.where(gas, F_LG, F_LL), jnp.where(gas, F_GG - F_LG, F_LG - F_LL)


def row_sums(parts):
    rows = []
    for part in parts:
        for sy in range(4):
            rows.append(jnp.sum(part[16 * sy : 16 * sy + 16], axis=0, keepdims=True))
    stacked = jnp.concatenate(rows, axis=0)
    pick = jnp.where(iota((128, 128), 0) // 32 == iota((128, 128), 1) % 4, 1.0, 0.0).astype(F32)
    spread = jnp.dot(stacked, pick, precision=EXACT, preferred_element_type=F32)
    keep = (iota((16, 128), 1) // 4) % 16 == iota((16, 128), 0)
    return jnp.sum(jnp.where(keep, spread, 0.0), axis=0, keepdims=True)


def fields(rows):
    count = len(rows)
    keep = (iota((16, 128), 1) // 4 == iota((16, 128), 0)) & (iota((16, 128), 1) < ND)
    tall = jnp.concatenate([jnp.where(keep, jnp.broadcast_to(r, (16, 128)), 0.0) for r in rows], axis=0)
    pick = jnp.where(iota((128, 128), 0) % 4 == iota((128, 128), 1) // 32, 1.0, 0.0).astype(F32)
    out = jnp.dot(tall, pick, precision=EXACT, preferred_element_type=F32)
    return [out[16 * k : 16 * k + 16] for k in range(count)]


def plane_field(field, sx):
    return jnp.concatenate(
        [jnp.broadcast_to(field[4 * sx + sy : 4 * sx + sy + 1], (16, 128)) for sy in range(4)], axis=0
    )


def coarse_rows(matrix_ref, even, odd):
    wide = jnp.where(iota((64, 128), 1) < ND, even, odd)
    total = matrix_ref[:, 0:128] * wide[0:1]
    for t in range(1, 64):
        total = total + matrix_ref[:, 128 * t : 128 * t + 128] * wide[t : t + 1]
    column = jnp.sum(total, axis=1, keepdims=True)
    keep = iota((64, 128), 1) % ND == iota((64, 128), 0)
    return jnp.sum(jnp.where(keep, column, 0.0), axis=0, keepdims=True)


def total_sum(x):
    return jnp.sum(jnp.sum(x, axis=0, keepdims=True), axis=1, keepdims=True)


def start_kernel(r_in, phase_in, v_in, xl_ref, xr_ref, send_ref, r_ref, g_ref, v_ref, phase_ref, sem):
    pairs = ((r_in, r_ref), (v_in, v_ref), (phase_in, phase_ref))
    copies = [pltpu.make_async_copy(src, dst, sem.at[n]) for n, (src, dst) in enumerate(pairs)]
    for copy in copies:
        copy.start()
    for copy in copies:
        copy.wait()
    parts = []
    for sx in range(4):
        parts.append(r_ref[2 * sx] * v_ref[2 * sx] + r_ref[2 * sx + 1] * v_ref[2 * sx + 1])
    send_ref[...] = jnp.broadcast_to(row_sums(parts), (NDEV, 128))
    xl_ref[0:H_R] = r_ref[0:H_R]
    xr_ref[0:H_R] = r_ref[CX - H_R :]
    g_ref[...] = jnp.where(phase_ref[...] == 1, 1.0, 0.0).astype(F32)
    xl_ref[H_R : H_R + H_G] = g_ref[0:H_G]
    xr_ref[H_R : H_R + H_G] = g_ref[CX - H_G :]
    xl_ref[H_R + H_G :] = v_ref[0:H_V]
    xr_ref[H_R + H_G :] = v_ref[CX - H_V :]


def stacked_planes(r_ref, g_ref, v_ref, fl_ref, fr_ref):
    planes = []
    for halo, own, base in ((H_R, "r", 0), (H_G, "g", H_R), (H_V, "v", H_R + H_G)):
        for rel in range(-halo, CX + halo):
            if rel < 0:
                planes.append(lambda s, k=base + rel + halo: fl_ref[k, s])
            elif rel >= CX:
                planes.append(lambda s, k=base + rel - CX: fr_ref[k, s])
            elif own == "r":
                planes.append(lambda s, k=rel: r_ref[k, s])
            elif own == "g":
                planes.append(lambda s, k=rel: g_ref[k, s])
            else:
                planes.append(lambda s, k=rel: v_ref[k, s])
    return planes


def y_kernel(r_ref, g_ref, v_ref, fl_ref, fr_ref, yl_ref, yr_ref):
    planes = stacked_planes(r_ref, g_ref, v_ref, fl_ref, fr_ref)
    for k, plane in enumerate(planes):
        yl_ref[k] = plane(pl.ds(0, HY))
        yr_ref[k] = plane(pl.ds(CY - HY, HY))


def pack_lanes(ext_ref, zl_ref, zr_ref, count):
    slot = iota((PY, CZ), 1) // 8
    for group in range(zl_ref.shape[0]):
        left = jnp.zeros((PY, CZ), F32)
        right = jnp.zeros((PY, CZ), F32)
        for m in range(16):
            k = 16 * group + m
            if k >= count:
                break
            plane = ext_ref[k]
            left = jnp.where(slot == m, pltpu.roll(plane, 8 * m, 1) if m else plane, left)
            shift = (8 * m + 8) % CZ
            right = jnp.where(slot == m, pltpu.roll(plane, shift, 1) if shift else plane, right)
        zl_ref[group] = left
        zr_ref[group] = right


def wide_plane(ext_ref, fl_ref, fr_ref, k):
    group, m = k // 16, k % 16
    lane = iota((PY, CZ), 1)
    shift = (CZ - 8 * m) % CZ
    ahead = pltpu.roll(fr_ref[group], shift, 1) if shift else fr_ref[group]
    shift = (CZ - 8 - 8 * m) % CZ
    behind = pltpu.roll(fl_ref[group], shift, 1) if shift else fl_ref[group]
    side = jnp.where(lane < 8, ahead, jnp.where(lane >= CZ - 8, behind, 0.0))
    return jnp.concatenate([ext_ref[k], side], axis=1)


def z_kernel(r_ref, g_ref, v_ref, fl_ref, fr_ref, yd_ref, yu_ref, ext_ref, zl_ref, zr_ref):
    planes = stacked_planes(r_ref, g_ref, v_ref, fl_ref, fr_ref)
    for k, plane in enumerate(planes):
        ext_ref[k, 0:HY] = yd_ref[k]
        ext_ref[k, HY : HY + CY] = plane(pl.ds(0, CY))
        ext_ref[k, HY + CY :] = yu_ref[k]
    pack_lanes(ext_ref, zl_ref, zr_ref, N_ALL)


def y2_kernel(p_ref, fl_ref, fr_ref, yl_ref, yr_ref):
    for i in range(PX):
        rel = i - HX
        src, k = (fl_ref, i) if rel < 0 else (fr_ref, rel - CX) if rel >= CX else (p_ref, rel)
        yl_ref[i] = src[k, 0:HY]
        yr_ref[i] = src[k, CY - HY :]


def z2_kernel(p_ref, fl_ref, fr_ref, yd_ref, yu_ref, ext_ref, zl_ref, zr_ref):
    for i in range(PX):
        rel = i - HX
        src, k = (fl_ref, i) if rel < 0 else (fr_ref, rel - CX) if rel >= CX else (p_ref, rel)
        ext_ref[i, 0:HY] = yd_ref[i]
        ext_ref[i, HY : HY + CY] = src[k]
        ext_ref[i, HY + CY :] = yu_ref[i]
    pack_lanes(ext_ref, zl_ref, zr_ref, PX)


def chebyshev(halo, w_ref, rp_ref, a_ref, b_ref):
    _, weights = recurrence()
    now, before = a_ref, b_ref
    for index, (keep, push) in enumerate(weights):
        halo -= 1
        for i in range(HX - halo, HX + CX + halo):
            for j in range(ROWS):
                around = around_strided(lambda i, j: now[i, j], i, j)
                total = rp_ref[i, j]
                for d in range(6):
                    total = total + w_ref[d, i, j] * around[d]
                new = (1.0 + keep - push) * now[i, j] + push * total
                if index:
                    new = new - keep * before[i, j]
                before[i, j] = new
        now, before = before, now
    return now


def smooth_kernel(pos, ext_ref, zl_ref, zr_ref, sums_ref, matrix_ref, p_ref, xl_ref, xr_ref, g_ref, v_ref, wide_ref, w_ref, rp_ref, a_ref, b_ref):
    mask = inside_yz(pos)
    for i in range(PX):
        put(g_ref, i, wide_plane(ext_ref, zl_ref, zr_ref, N_R + i) * (mask * inside_x(pos, i - HX)))
    for i in range(N_V):
        put(v_ref, i, wide_plane(ext_ref, zl_ref, zr_ref, N_R + N_G + i) * (mask * inside_x(pos, i - H_V)))
    for k in range(N_R):
        put(wide_ref, k, wide_plane(ext_ref, zl_ref, zr_ref, k))
    first_scale, _ = recurrence()
    for j in range(ROWS):
        mask = inside_yz(pos, j)
        for i in range(HX - H_R, HX + CX + H_R):
            labels = around_strided(lambda i, j: strided(g_ref, i, j), i, j)
            first, second = pair(strided(g_ref, i, j))
            count = (labels[0] + labels[1]) + (labels[2] + labels[3]) + (labels[4] + labels[5])
            inverse = mask * inside_x(pos, i - HX) / (6.0 * first + second * count)
            first, second = first * inverse, second * inverse
            for d in range(6):
                w_ref[d, i, j] = first + second * labels[d]
            scaled = strided(wide_ref, i - HX + H_R, j) * inverse
            rp_ref[i, j] = scaled
            a_ref[i, j] = scaled * first_scale
    result = chebyshev(H_R, w_ref, rp_ref, a_ref, b_ref)
    for x in range(CX):
        for j in range(ROWS):
            wide_ref[0, x, pl.ds(j, 8, stride=ROWS), :] = result[HX + x, j, :, 0:CZ]
    even = sums_ref[pl.ds(0, 64, stride=2), :]
    odd = sums_ref[pl.ds(1, 64, stride=2), :]
    amounts = coarse_rows(matrix_ref, even, odd)
    (field,) = fields([amounts])
    for x in range(CX):
        value = wide_ref[0, x, HY : HY + CY]
        value = value + v_ref[0, x + H_V, HY : HY + CY] * plane_field(field, x // 2)
        p_ref[x] = value
        if x < HX:
            xl_ref[x] = value
        if x >= CX - HX:
            xr_ref[x - CX + HX] = value


def product_kernel(g_ref, v_ref, out_ref):
    last_y = iota((CY, CZ), 0) % 16 == 15
    last_z = iota((CY, CZ), 1) % 32 == 31
    quads = [[], [], [], []]

    def own(a):
        return a[HY : HY + CY, 0:CZ]

    for sx in range(4):
        sums = [jnp.zeros((CY, CZ), F32) for _ in range(4)]
        for x in (2 * sx, 2 * sx + 1):
            labels = neighbours(g_ref, x + HX)
            values = neighbours(v_ref, x + H_V)
            first, second = pair(own(whole(g_ref, x + HX)))
            mine = own(whole(v_ref, x + H_V))
            count = sum(own(a) for a in labels)
            sums[0] = sums[0] + (6.0 * first + second * count) * mine * mine
            cross = [(first + second * own(labels[d])) * mine * own(values[d]) for d in (1, 3, 5)]
            if x % 2 == 0:
                sums[0] = sums[0] - 2.0 * cross[0]
            else:
                sums[1] = sums[1] - cross[0]
            sums[0] = sums[0] - 2.0 * jnp.where(last_y, 0.0, cross[1]) - 2.0 * jnp.where(last_z, 0.0, cross[2])
            sums[2] = sums[2] - jnp.where(last_y, cross[1], 0.0)
            sums[3] = sums[3] - jnp.where(last_z, cross[2], 0.0)
        for n in range(4):
            quads[n].append(sums[n])
    for n in range(4):
        out_ref[n : n + 1] = row_sums(quads[n])


def image_plane(ref, i, first, second, labels):
    mine = whole(ref, i)
    around = neighbours(ref, i)
    total = (first + second * labels[0]) * (mine - around[0])
    for d in range(1, 6):
        total = total + (first + second * labels[d]) * (mine - around[d])
    return total


def image_kernel(
    pos, ext_ref, zl_ref, zr_ref, g_ref, r_ref, v_ref, e_ref, q_ref, c_ref, y_ref, send_ref, full_ref, plane_ref, w_ref, rp_ref, a_ref, b_ref
):
    mask = inside_yz(pos)
    for i in range(PX):
        put(full_ref, i, wide_plane(ext_ref, zl_ref, zr_ref, i) * (mask * inside_x(pos, i - HX)))
    first_scale, _ = recurrence()
    for j in range(ROWS):
        mask = inside_yz(pos, j)
        for i in range(1, PX - 1):
            labels = around_strided(lambda i, j: strided(g_ref, i, j), i, j)
            values = around_strided(lambda i, j: strided(full_ref, i, j), i, j)
            first, second = pair(strided(g_ref, i, j))
            count = (labels[0] + labels[1]) + (labels[2] + labels[3]) + (labels[4] + labels[5])
            inverse = mask * inside_x(pos, i - HX) / (6.0 * first + second * count)
            mine = strided(full_ref, i, j)
            image = jnp.zeros_like(mine)
            for d in range(6):
                face = first + second * labels[d]
                image = image + face * (mine - values[d])
                w_ref[d, i, j] = face * inverse
            if HX <= i < HX + CX:
                plane_ref[i - HX, pl.ds(j, 8, stride=ROWS), :] = image[:, 0:CZ]
            scaled = image * inverse
            rp_ref[i, j] = scaled
            a_ref[i, j] = scaled * first_scale
    parts = []
    energy = jnp.zeros((CY, CZ), F32)
    curve = jnp.zeros((CY, CZ), F32)
    for x in range(CX):
        image = plane_ref[x, HY : HY + CY]
        value = full_ref[0, HX + x, HY : HY + CY]
        q_ref[x] = image
        energy = energy + r_ref[x] * value
        curve = curve + image * value
        term = v_ref[x] * image
        if x % 2 == 0:
            parts.append(term)
        else:
            parts[-1] = parts[-1] + term
    result = chebyshev(HX - 1, w_ref, rp_ref, a_ref, b_ref)
    for x in range(CX):
        i = HX + x
        for j in range(ROWS):
            labels = around_strided(lambda i, j: strided(g_ref, i, j), i, j)
            values = around_strided(lambda i, j: result[i, j], i, j)
            first, second = pair(strided(g_ref, i, j))
            mine = result[i, j]
            image = jnp.zeros_like(mine)
            for d in range(6):
                image = image + (first + second * labels[d]) * (mine - values[d])
            full_ref[0, x, pl.ds(j, 8, stride=ROWS), :] = mine[:, 0:CZ]
            plane_ref[x, pl.ds(j, 8, stride=ROWS), :] = image[:, 0:CZ]
        c_ref[x] = full_ref[0, x, HY : HY + CY]
        y_ref[x] = plane_ref[x, HY : HY + CY]
    lane = iota((1, 128), 1)
    scalars = jnp.where(lane == 64, total_sum(energy), jnp.where(lane == 65, total_sum(curve), 0.0))
    send = jnp.concatenate(
        [
            jnp.where(lane < ND, row_sums(parts), e_ref[0:1]),
            jnp.where(lane < ND, e_ref[1:2], e_ref[2:3]),
            jnp.where(lane < ND, e_ref[3:4], scalars),
        ],
        axis=1,
    )
    send_ref[...] = jnp.broadcast_to(send, (NDEV, 384))


def first_scalars(sums_ref):
    totals = jnp.sum(sums_ref[:, 256:384], axis=0, keepdims=True)
    energy = totals[0:1, 64:65]
    curve = totals[0:1, 65:66]
    return energy, curve, energy / curve


def amounts_kernel(sums_ref, matrix_ref, p_ref, q_ref, c_ref, y_ref, v_ref, r_ref, send_ref, piece_ref):
    _, _, alpha = first_scalars(sums_ref)
    piece_ref[...] = sums_ref[:, 0:128]
    even = piece_ref[pl.ds(0, 64, stride=2), :]
    odd = pltpu.roll(piece_ref[pl.ds(1, 64, stride=2), :], 64, 1)
    amounts = coarse_rows(matrix_ref, even, odd)
    (field,) = fields([amounts])
    sums = [jnp.zeros((CY, CZ), F32) for _ in range(3)]
    for x in range(CX):
        lifted = v_ref[x] * plane_field(field, x // 2)
        p, q, c = p_ref[x], q_ref[x], c_ref[x]
        residual = r_ref[x] - alpha * q
        smooth = p - alpha * c
        smooth_image = q - alpha * y_ref[x]
        precond = smooth - alpha * lifted
        sums[0] = sums[0] + residual * precond
        sums[1] = sums[1] + precond * q
        sums[2] = sums[2] + smooth_image * (smooth - 2.0 * alpha * lifted)
    lane = iota((1, 128), 1)
    row = jnp.where(lane < ND, amounts, 0.0)
    for n in range(3):
        row = jnp.where(lane == ND + n, total_sum(sums[n]), row)
    send_ref[...] = jnp.broadcast_to(row, (NDEV, 128))


def final_kernel(
    pos, sums_ref, got_ref, p_ref, q_ref, c_ref, y_ref, r_ref, vx_ref, g_ref, pressure_ref, residual_ref, lift_ref
):
    energy, curve, alpha = first_scalars(sums_ref)
    got = got_ref[...]
    lane = iota((NDEV, 128), 1)
    dup = jnp.where(lane < ND, got, pltpu.roll(got, 64, 1))
    sz, sy, sx = lane % 4, (lane // 4) % 4, (lane // 16) % 4
    next_z = jnp.where(sz < 3, pltpu.roll(dup, 127, 1), pltpu.roll(pltpu.roll(dup, 3, 1), NDEV - 1, 0))
    next_y = jnp.where(sy < 3, pltpu.roll(dup, 124, 1), pltpu.roll(pltpu.roll(dup, 12, 1), NDEV - 8, 0))
    next_x = jnp.where(sx < 3, pltpu.roll(dup, 112, 1), pltpu.roll(pltpu.roll(dup, 48, 1), NDEV - 32, 0))
    one, two = sums_ref[:, 0:128], sums_ref[:, 128:256]
    three = sums_ref[:, 256:384]
    half = dup * pltpu.roll(one, 64, 1) + 2.0 * (next_x * two + next_y * pltpu.roll(two, 64, 1) + next_z * three)
    quad = total_sum(jnp.where(lane < ND, half * dup, 0.0))
    totals = jnp.sum(got, axis=0, keepdims=True)
    energy_next = totals[0:1, 64:65]
    mixed = totals[0:1, 65:66]
    beta = energy_next / energy
    curve_next = totals[0:1, 66:67] + alpha * alpha * quad + 2.0 * beta * mixed + beta * beta * curve
    alpha_next = energy_next / curve_next

    me = (pos[0] * 4 + pos[1]) * 8 + pos[2]
    rows = []
    for shift in (0, -32, 32, -8, 8, -1, 1):
        at = jnp.clip(me + shift, 0, NDEV - 1)
        rows.append(got_ref[pl.ds(at, 1), :])
    mine, xm, xp, ym, yp, zm, zp = fields(rows)
    lanes = iota((PY, CZ), 1)
    zeros = jnp.zeros((HY, CZ), F32)
    for i in range(N_V):
        x = i - H_V
        if x < 0 or x >= CX:
            own = plane_field(xm, 3) if x < 0 else plane_field(xp, 0)
            middle = jnp.concatenate([zeros, own, zeros], axis=0)
            side = jnp.zeros((PY, CZ), F32)
        else:
            s = x // 2
            down = jnp.broadcast_to(ym[4 * s + 3 : 4 * s + 4], (HY, CZ))
            up = jnp.broadcast_to(yp[4 * s : 4 * s + 1], (HY, CZ))
            middle = jnp.concatenate([down, plane_field(mine, s), up], axis=0)
            ahead = jnp.concatenate([zeros, plane_field(zp, s), zeros], axis=0)
            behind = jnp.concatenate([zeros, plane_field(zm, s), zeros], axis=0)
            side = jnp.where(lanes < 8, ahead, jnp.where(lanes >= CZ - 8, behind, 0.0))
        lift_ref[0, i] = vx_ref[0, i] * middle
        lift_ref[1, i] = vx_ref[1, i] * side
    for x in range(CX):
        first, second = pair(whole(g_ref, x + HX))
        lifted_image = image_plane(lift_ref, x + H_V, first, second, neighbours(g_ref, x + HX))
        lifted_image = lifted_image[HY : HY + CY, 0:CZ]
        lifted = lift_ref[0, x + H_V, HY : HY + CY]
        p, q = p_ref[x], q_ref[x]
        precond = p - alpha * (c_ref[x] + lifted)
        precond_image = q - alpha * (y_ref[x] + lifted_image)
        direction = precond + beta * p
        image = precond_image + beta * q
        pressure_ref[x] = alpha * p + alpha_next * direction
        residual_ref[x] = (r_ref[x] - alpha * q) - alpha_next * image


VMEM = pl.BlockSpec(memory_space=pltpu.VMEM)
SMEM = pl.BlockSpec(memory_space=pltpu.SMEM)


def call(kernel, outs, scratch=(), smem=False, hbm=0, mib=48, cost=None):
    def run(*args):
        many = isinstance(outs, list)
        specs = [VMEM] * len(args)
        if smem:
            specs[0] = SMEM
        for n in range(hbm):
            specs[n] = pl.BlockSpec(memory_space=pltpu.HBM)
        return pl.pallas_call(
            kernel,
            out_shape=[jax.ShapeDtypeStruct(s, F32) for s in outs] if many else jax.ShapeDtypeStruct(outs, F32),
            in_specs=specs,
            out_specs=[VMEM] * len(outs) if many else VMEM,
            scratch_shapes=[pltpu.VMEM(s, F32) if isinstance(s, tuple) else s for s in scratch],
            compiler_params=pltpu.CompilerParams(vmem_limit_bytes=mib * 1024 * 1024),
            cost_estimate=cost,
        )(*args)

    return run


def cost(us):
    return pl.CostEstimate(flops=int(us * 1e6), bytes_accessed=int(us * 3e6), transcendentals=0)


def swap(to_left, to_right, axis):
    count = lax.axis_size(axis)
    from_right = lax.ppermute(to_left, axis, [((i + 1) % count, i) for i in range(count)])
    from_left = lax.ppermute(to_right, axis, [(i, (i + 1) % count) for i in range(count)])
    return from_left, from_right


def gather(rows):
    return lax.all_to_all(rows, AXES, 0, 0, tiled=True)


def local(right_side, phase, deflation_weights, coarse_inverse):
    pos = jnp.stack([lax.axis_index(a) for a in AXES]).astype(jnp.int32)
    block = (CX, CY, CZ)
    tall = (2, PX, PY, CZ)
    split = (PX, ROWS, 8, PZ)
    n_x = H_R + H_G + H_V
    xl, xr, send, r, g, v = call(
        start_kernel,
        [(n_x, CY, CZ), (n_x, CY, CZ), (NDEV, 128), block, block, block],
        scratch=[pltpu.VMEM(block, jnp.int32), pltpu.SemaphoreType.DMA((3,))],
        hbm=3,
    )(right_side, phase, deflation_weights)
    fl, fr = swap(xl, xr, "gx")
    sums = gather(send)
    fl, fr, sums = lax.optimization_barrier((fl, fr, sums))
    yl, yr = call(y_kernel, [(N_ALL, HY, CZ)] * 2)(r, g, v, fl, fr)
    yd, yu = swap(yl, yr, "gy")
    ext, zl, zr = call(z_kernel, [(N_ALL, PY, CZ), (GROUPS, PY, CZ), (GROUPS, PY, CZ)])(r, g, v, fl, fr, yd, yu)
    zfl, zfr = swap(zl, zr, "gz")
    p, xl, xr, labels, v_wide = call(
        smooth_kernel,
        [block, (HX, CY, CZ), (HX, CY, CZ), tall, (2, N_V, PY, CZ)],
        scratch=[(2, N_R, PY, CZ), (6, *split), split, split, split],
        smem=True,
    )(pos, ext, zfl, zfr, sums, coarse_inverse)
    fl, fr = swap(xl, xr, "gx")
    quads = call(product_kernel, (4, 128), cost=cost(1))(
        labels, v_wide
    )
    yl, yr = call(y2_kernel, [(PX, HY, CZ)] * 2)(p, fl, fr)
    yd, yu = swap(yl, yr, "gy")
    ext, zl, zr = call(z2_kernel, [(PX, PY, CZ), (GROUPS_P, PY, CZ), (GROUPS_P, PY, CZ)])(p, fl, fr, yd, yu)
    zfl, zfr = swap(zl, zr, "gz")
    q, c, y, send = call(
        image_kernel,
        [block, block, block, (NDEV, 384)],
        scratch=[tall, (CX, PY, CZ), (6, *split), split, split, split],
        smem=True,
    )(pos, ext, zfl, zfr, labels, r, v, quads)
    sums = gather(send)
    send = call(amounts_kernel, (NDEV, 128), scratch=[(NDEV, 128)])(sums, coarse_inverse, p, q, c, y, v, r)
    got = gather(send)
    pressure, residual = call(final_kernel, [block, block], scratch=[(2, N_V, PY, CZ)], smem=True)(
        pos, sums, got, p, q, c, y, r, v_wide, labels
    )
    return (pressure, residual)


def solution(mesh):
    return jax.shard_map(
        local,
        mesh=mesh,
        in_specs=(P(*AXES), P(*AXES), P(*AXES), P(AXES, None)),
        out_specs=(P(*AXES), P(*AXES)),
        check_vma=False,
    )
```

```python
import functools

import jax
import jax.numpy as jnp
import numpy as np
from jax import lax
from jax.experimental import pallas as pl
from jax.experimental.pallas import tpu as pltpu
from jax.sharding import PartitionSpec as P

AXES = ("gx", "gy", "gz")
SBX = 4
ND = 64
DEG = 6
spectrum_low = 0.08
spectrum_high = 2.0

CX, CY, CZ = 8, 64, 128
HX, HY = 7, 8
PX, PY, PZ = CX + 2 * HX, CY + 2 * HY, 2 * CZ
H_R, H_G, H_V = 5, 7, 1
N_R, N_G, N_V = CX + 2 * H_R, CX + 2 * H_G, CX + 2 * H_V
N_ALL = N_R + N_G + N_V
GROUPS = -(-N_ALL // 16)
GROUPS_P = -(-PX // 16)
NDEV = 128
ROWS = PY // 8

LIQUID = np.float32(1.0)
GAS = np.float32(0.001)
F_LL = np.float32(2.0) / (LIQUID + LIQUID)
F_LG = np.float32(2.0) / (LIQUID + GAS)
F_GG = np.float32(2.0) / (GAS + GAS)

F32 = jnp.float32
EXACT = lax.Precision.HIGHEST


def recurrence():
    center = 0.5 * (spectrum_high + spectrum_low)
    half_width = 0.5 * (spectrum_high - spectrum_low)
    ratio = center / half_width
    earlier = 1.0 / ratio
    weights = []
    for index in range(DEG - 1):
        later = 1.0 / (2.0 * ratio - earlier)
        weights.append((later * earlier, 2.0 * later / half_width))
        earlier = later
    return (1.0 / center, weights)


def iota(shape, dim):
    return lax.broadcasted_iota(jnp.int32, shape, dim)


def whole(ref, i):
    return jnp.concatenate([ref[0, i], ref[1, i]], axis=1)


def put(ref, i, plane):
    ref[0, i] = plane[:, 0:CZ]
    ref[1, i] = plane[:, CZ:PZ]


def neighbours(ref, i):
    v = whole(ref, i)
    return (
        whole(ref, i - 1),
        whole(ref, i + 1),
        pltpu.roll(v, 1, 0),
        pltpu.roll(v, PY - 1, 0),
        pltpu.roll(v, 1, 1),
        pltpu.roll(v, PZ - 1, 1),
    )


def strided(ref, i, j):
    rows = pl.ds(j, 8, stride=ROWS)
    return jnp.concatenate([ref[0, i, rows, :], ref[1, i, rows, :]], axis=1)


def around_strided(load, i, j):
    v = load(i, j)
    return (
        load(i - 1, j),
        load(i + 1, j),
        load(i, j - 1) if j else pltpu.roll(load(i, ROWS - 1), 1, 0),
        load(i, j + 1) if j < ROWS - 1 else pltpu.roll(load(i, 0), 7, 0),
        pltpu.roll(v, 1, 1),
        pltpu.roll(v, PZ - 1, 1),
    )


def inside_yz(pos, j=None):
    gy, gz = pos[1], pos[2]
    shape = (PY, PZ) if j is None else (8, PZ)
    row = iota(shape, 0) if j is None else iota(shape, 0) * ROWS + j
    row = row - HY + gy * CY
    lane = iota(shape, 1)
    near = jnp.where(lane < CZ + CZ // 2, lane, lane - PZ) + gz * CZ
    kept = (lane < CZ + 8) | (lane >= PZ - 8)
    good = (row >= 0) & (row < 4 * CY) & (near >= 0) & (near < 8 * CZ) & kept
    return jnp.where(good, 1.0, 0.0).astype(F32)


def inside_x(pos, rel):
    x = pos[0] * CX + rel
    return jnp.where((x >= 0) & (x < 4 * CX), 1.0, 0.0).astype(F32)


def pair(labels):
    gas = labels > 0.5
    return jnp.where(gas, F_LG, F_LL), jnp.where(gas, F_GG - F_LG, F_LG - F_LL)


def row_sums(arrays):
    rows = []
    for parts in arrays:
        for part in parts:
            for sy in range(4):
                rows.append(jnp.sum(part[16 * sy : 16 * sy + 16], axis=0, keepdims=True))
    stacked = jnp.concatenate(rows, axis=0)
    pick = jnp.where(iota((128, 128), 0) // 32 == iota((128, 128), 1) % 4, 1.0, 0.0).astype(F32)
    spread = jnp.dot(stacked, pick, precision=EXACT, preferred_element_type=F32)
    keep = (iota((16, 128), 1) // 4) % 16 == iota((16, 128), 0)
    return [
        jnp.sum(jnp.where(keep, spread[16 * n : 16 * n + 16], 0.0), axis=0, keepdims=True) for n in range(len(arrays))
    ]


def fields(rows):
    count = len(rows)
    keep = (iota((16, 128), 1) // 4 == iota((16, 128), 0)) & (iota((16, 128), 1) < ND)
    tall = jnp.concatenate([jnp.where(keep, jnp.broadcast_to(r, (16, 128)), 0.0) for r in rows], axis=0)
    pick = jnp.where(iota((128, 128), 0) % 4 == iota((128, 128), 1) // 32, 1.0, 0.0).astype(F32)
    out = jnp.dot(tall, pick, precision=EXACT, preferred_element_type=F32)
    return [out[16 * k : 16 * k + 16] for k in range(count)]


def plane_field(field, sx):
    return jnp.concatenate(
        [jnp.broadcast_to(field[4 * sx + sy : 4 * sx + sy + 1], (16, 128)) for sy in range(4)], axis=0
    )


def coarse_rows(matrix_ref, even, odd):
    wide = jnp.where(iota((64, 128), 1) < ND, even, odd)
    total = matrix_ref[:, 0:128] * wide[0:1]
    for t in range(1, 64):
        total = total + matrix_ref[:, 128 * t : 128 * t + 128] * wide[t : t + 1]
    column = jnp.sum(total, axis=1, keepdims=True)
    keep = iota((64, 128), 1) % ND == iota((64, 128), 0)
    return jnp.sum(jnp.where(keep, column, 0.0), axis=0, keepdims=True)


def total_sum(x):
    return jnp.sum(jnp.sum(x, axis=0, keepdims=True), axis=1, keepdims=True)


def start_kernel(pos, r_in, phase_in, v_in, xa_ref, xb_ref, send_ref, r_ref, g_ref, v_ref, phase_ref, sem):
    pairs = ((r_in, r_ref), (v_in, v_ref), (phase_in, phase_ref))
    copies = [pltpu.make_async_copy(src, dst, sem.at[n]) for n, (src, dst) in enumerate(pairs)]
    for copy in copies:
        copy.start()
    for copy in copies:
        copy.wait()
    parts = []
    for sx in range(4):
        parts.append(r_ref[2 * sx] * v_ref[2 * sx] + r_ref[2 * sx + 1] * v_ref[2 * sx + 1])
    (row,) = row_sums([parts])
    send_ref[...] = jnp.broadcast_to(row, (NDEV, 128))
    g_ref[...] = jnp.where(phase_ref[...] == 1, 1.0, 0.0).astype(F32)
    even = is_even(pos, 0)
    for base, ref, halo in ((0, r_ref, H_R), (H_R, g_ref, H_G), (H_R + H_G, v_ref, H_V)):
        for k in range(halo):
            put_pair(even, xa_ref, xb_ref, base + k, ref[k], ref[CX - halo + k])


def is_even(pos, axis):
    return (pos[axis] & 1) == 0


def put_pair(even, a_ref, b_ref, k, down, up):
    a_ref[k] = jnp.where(even, up, down)
    b_ref[k] = jnp.where(even, down, up)


class Pair:
    def __init__(self, pos, axis, a_ref, b_ref):
        self.even, self.a, self.b = is_even(pos, axis), a_ref, b_ref

    def below(self, *at):
        return jnp.where(self.even, self.b[at], self.a[at])

    def above(self, *at):
        return jnp.where(self.even, self.a[at], self.b[at])


def stacked_planes(r_ref, g_ref, v_ref, sides):
    planes = []
    for halo, ref, base in ((H_R, r_ref, 0), (H_G, g_ref, H_R), (H_V, v_ref, H_R + H_G)):
        for rel in range(-halo, CX + halo):
            if rel < 0:
                planes.append(lambda s, k=base + rel + halo: sides.below(k, s))
            elif rel >= CX:
                planes.append(lambda s, k=base + rel - CX: sides.above(k, s))
            else:
                planes.append(lambda s, k=rel, ref=ref: ref[k, s])
    return planes


def padded_planes(p_ref, sides):
    planes = []
    for rel in range(-HX, CX + HX):
        if rel < 0:
            planes.append(lambda s, k=rel + HX: sides.below(k, s))
        elif rel >= CX:
            planes.append(lambda s, k=rel - CX: sides.above(k, s))
        else:
            planes.append(lambda s, k=rel: p_ref[k, s])
    return planes


def all_planes(refs, pos):
    sides = Pair(pos, 0, *refs[-2:])
    return padded_planes(refs[0], sides) if len(refs) == 3 else stacked_planes(*refs[:3], sides)


def y_kernel(pos, *refs):
    even = is_even(pos, 1)
    for k, plane in enumerate(all_planes(refs[:-2], pos)):
        put_pair(even, *refs[-2:], k, plane(pl.ds(0, HY)), plane(pl.ds(CY - HY, HY)))


def pack_lanes(values, rows):
    slot = iota((rows, CZ), 1) // 8
    packed = []
    for base in range(0, len(values), 16):
        left = right = jnp.zeros((rows, CZ), F32)
        for m, value in enumerate(values[base : base + 16]):
            value = value()
            left = jnp.where(slot == m, pltpu.roll(value, 8 * m, 1) if m else value, left)
            shift = (8 * m + 8) % CZ
            right = jnp.where(slot == m, pltpu.roll(value, shift, 1) if shift else value, right)
        packed.append((left, right))
    return packed


def z_own_kernel(pos, *refs):
    planes = all_planes(refs[:-2], pos)
    values = [lambda plane=plane: plane(pl.ds(0, CY)) for plane in planes]
    for group, (left, right) in enumerate(pack_lanes(values, CY)):
        refs[-2][group] = left
        refs[-1][group] = right


def z_kernel(pos, ya_ref, yb_ref, left_ref, right_ref, za_ref, zb_ref):
    even = is_even(pos, 2)
    sides = Pair(pos, 1, ya_ref, yb_ref)
    count = ya_ref.shape[0]
    below = pack_lanes([lambda k=k: sides.below(k) for k in range(count)], HY)
    above = pack_lanes([lambda k=k: sides.above(k) for k in range(count)], HY)
    for group in range(len(below)):
        left = jnp.concatenate([below[group][0], left_ref[group], above[group][0]], axis=0)
        right = jnp.concatenate([below[group][1], right_ref[group], above[group][1]], axis=0)
        put_pair(even, za_ref, zb_ref, group, left, right)


class Wide:
    def __init__(self, planes, pos, ya_ref, yb_ref, za_ref, zb_ref):
        self.planes = planes
        self.y = Pair(pos, 1, ya_ref, yb_ref)
        z = Pair(pos, 2, za_ref, zb_ref)
        groups = za_ref.shape[0]
        self.behind = [z.below(g) for g in range(groups)]
        self.ahead = [z.above(g) for g in range(groups)]

    def __call__(self, k):
        group, m = k // 16, k % 16
        lane = iota((PY, CZ), 1)
        shift = (CZ - 8 * m) % CZ
        ahead = pltpu.roll(self.ahead[group], shift, 1) if shift else self.ahead[group]
        shift = (CZ - 8 - 8 * m) % CZ
        behind = pltpu.roll(self.behind[group], shift, 1) if shift else self.behind[group]
        side = jnp.where(lane < 8, ahead, jnp.where(lane >= CZ - 8, behind, 0.0))
        middle = jnp.concatenate([self.y.below(k), self.planes[k](pl.ds(0, CY)), self.y.above(k)], axis=0)
        return jnp.concatenate([middle, side], axis=1)


def first_amounts_kernel(sums_ref, matrix_ref, out_ref):
    out_ref[...] = coarse_rows(matrix_ref, sums_ref[pl.ds(0, 64, stride=2), :], sums_ref[pl.ds(1, 64, stride=2), :])


def chebyshev(halo, w_ref, rp_ref, a_ref, b_ref):
    _, weights = recurrence()
    now, before = a_ref, b_ref
    for index, (keep, push) in enumerate(weights):
        halo -= 1
        for i in range(HX - halo, HX + CX + halo):
            for j in range(ROWS):
                around = around_strided(lambda i, j: now[i, j], i, j)
                total = rp_ref[i, j]
                for d in range(6):
                    total = total + w_ref[d, i, j] * around[d]
                new = (1.0 + keep - push) * now[i, j] + push * total
                if index:
                    new = new - keep * before[i, j]
                before[i, j] = new
        now, before = before, now
    return now


def smooth_kernel(
    pos, r_ref, g_in, v_in, xa_ref, xb_ref, ya_ref, yb_ref, za_ref, zb_ref, amounts_ref,
    p_ref, xa_out, xb_out, vx_ref, w_ref, diag_ref,
    g_ref, wide_ref, rp_ref, a_ref, b_ref, nat_ref,
):
    wide = Wide(stacked_planes(r_ref, g_in, v_in, Pair(pos, 0, xa_ref, xb_ref)), pos, ya_ref, yb_ref, za_ref, zb_ref)
    mask = inside_yz(pos)
    for i in range(PX):
        put(g_ref, i, wide(N_R + i) * (mask * inside_x(pos, i - HX)))
    for i in range(N_V):
        put(vx_ref, i, wide(N_R + N_G + i) * (mask * inside_x(pos, i - H_V)))
    for k in range(N_R):
        put(wide_ref, k, wide(k))
    first_scale, _ = recurrence()
    for j in range(ROWS):
        mask = inside_yz(pos, j)
        for i in range(1, PX - 1):
            labels = around_strided(lambda i, j: strided(g_ref, i, j), i, j)
            first, second = pair(strided(g_ref, i, j))
            count = (labels[0] + labels[1]) + (labels[2] + labels[3]) + (labels[4] + labels[5])
            diagonal = 6.0 * first + second * count
            if HX <= i < HX + CX:
                diag_ref[i - HX, j] = diagonal[:, 0:CZ]
            inverse = mask * inside_x(pos, i - HX) / diagonal
            first, second = first * inverse, second * inverse
            for d in range(6):
                w_ref[d, i, j] = first + second * labels[d]
            if HX - H_R <= i < HX + CX + H_R:
                scaled = strided(wide_ref, i - HX + H_R, j) * inverse
                rp_ref[i, j] = scaled
                a_ref[i, j] = scaled * first_scale
    result = chebyshev(H_R, w_ref, rp_ref, a_ref, b_ref)
    for j in range(ROWS):
        for x in range(CX):
            nat_ref[x, pl.ds(j, 8, stride=ROWS), :] = result[HX + x, j, :, 0:CZ]
    (field,) = fields([amounts_ref[...]])
    for x in range(CX):
        p_ref[x] = nat_ref[x, HY : HY + CY] + v_in[x] * plane_field(field, x // 2)
    even = is_even(pos, 0)
    for k in range(HX):
        put_pair(even, xa_out, xb_out, k, p_ref[k], p_ref[CX - HX + k])


def product_kernel(vx_ref, w_ref, diag_ref, out_ref, acc_ref):
    for j in range(ROWS):
        rows = pl.ds(j, 8, stride=ROWS)
        last_y = (iota((8, CZ), 0) * ROWS + j - HY) % 16 == 15
        last_z = iota((8, CZ), 1) % 32 == 31
        for sx in range(4):
            sums = [jnp.zeros((8, CZ), F32) for _ in range(4)]
            for x in (2 * sx, 2 * sx + 1):
                mine = strided(vx_ref, x + H_V, j)
                ahead = (
                    strided(vx_ref, x + H_V + 1, j),
                    strided(vx_ref, x + H_V, j + 1) if j < ROWS - 1 else pltpu.roll(strided(vx_ref, x + H_V, 0), 7, 0),
                    pltpu.roll(mine, PZ - 1, 1),
                )
                scaled = diag_ref[x, j] * mine[:, 0:CZ]
                cross = [scaled * w_ref[2 * d + 1, x + HX, j, :, 0:CZ] * ahead[d][:, 0:CZ] for d in range(3)]
                inner = jnp.where(last_y, 0.0, cross[1]) + jnp.where(last_z, 0.0, cross[2])
                if x % 2 == 0:
                    inner = inner + cross[0]
                else:
                    sums[1] = sums[1] - cross[0]
                sums[0] = sums[0] + (scaled * mine[:, 0:CZ] - 2.0 * inner)
                sums[2] = sums[2] - jnp.where(last_y, cross[1], 0.0)
                sums[3] = sums[3] - jnp.where(last_z, cross[2], 0.0)
            for n in range(4):
                acc_ref[4 * n + sx, rows, :] = sums[n]
    quads = row_sums([[acc_ref[4 * n + sx, HY : HY + CY] for sx in range(4)] for n in range(4)])
    for n in range(4):
        out_ref[n : n + 1] = quads[n]


def image_of(ref, w_ref, diag_ref, x, j):
    values = around_strided(lambda i, j: ref[i, j], x + HX, j)
    mine = ref[x + HX, j]
    total = w_ref[0, x + HX, j] * (mine - values[0])
    for d in range(1, 6):
        total = total + w_ref[d, x + HX, j] * (mine - values[d])
    return mine[:, 0:CZ], total[:, 0:CZ] * diag_ref[x, j]


def twice(x, half):
    lane = iota(x.shape, 1)
    other = pltpu.roll(x, ND, 1)
    return jnp.where(lane < ND, x, other) if half == 0 else jnp.where(lane < ND, other, x)


def ahead_behind(x, step, sign):
    lane = iota(x.shape, 1)
    stride, devices = ((16, 32), (4, 8), (1, 1))[step]
    place = (lane // stride) % 4
    near = pltpu.roll(x, (128 - stride * sign) % 128, 1)
    far = pltpu.roll(x, (3 * stride * sign) % 128, 1)
    far = pltpu.roll(far, (NDEV - devices * sign) % NDEV, 0)
    return jnp.where(place != (3 if sign > 0 else 0), near, far)


def image_kernel(
    pos, p_ref, xa_ref, xb_ref, ya_ref, yb_ref, za_ref, zb_ref, w_ref, diag_ref, r_ref, v_ref, e_ref,
    q_ref, c_ref, y_ref, send_ref,
    full_ref, plane_ref, rp_ref, a_ref, b_ref,
):
    wide = Wide(padded_planes(p_ref, Pair(pos, 0, xa_ref, xb_ref)), pos, ya_ref, yb_ref, za_ref, zb_ref)
    mask = inside_yz(pos)
    for i in range(PX):
        put(full_ref, i, wide(i) * (mask * inside_x(pos, i - HX)))
    first_scale, _ = recurrence()
    for j in range(ROWS):
        rows = pl.ds(j, 8, stride=ROWS)
        for i in range(1, PX - 1):
            values = around_strided(lambda i, j: strided(full_ref, i, j), i, j)
            mine = strided(full_ref, i, j)
            total = w_ref[0, i, j] * (mine - values[0])
            for d in range(1, 6):
                total = total + w_ref[d, i, j] * (mine - values[d])
            rp_ref[i, j] = total
            a_ref[i, j] = total * first_scale
            if HX <= i < HX + CX:
                plane_ref[i - HX, rows, :] = total[:, 0:CZ] * diag_ref[i - HX, j]
    result = chebyshev(HX - 1, w_ref, rp_ref, a_ref, b_ref)
    for x in range(CX):
        for j in range(ROWS):
            rows = pl.ds(j, 8, stride=ROWS)
            mine, image = image_of(result, w_ref, diag_ref, x, j)
            plane_ref[CX + x, rows, :] = mine
            plane_ref[2 * CX + x, rows, :] = image
    parts = [jnp.zeros((CY, CZ), F32) for _ in range(4)]
    energy = jnp.zeros((CY, CZ), F32)
    curve = jnp.zeros((CY, CZ), F32)
    for x in range(CX):
        q, c, y = (plane_ref[CX * n + x, HY : HY + CY] for n in range(3))
        q_ref[x], c_ref[x], y_ref[x] = q, c, y
        energy = energy + r_ref[x] * p_ref[x]
        curve = curve + q * p_ref[x]
        parts[x // 2] = parts[x // 2] + v_ref[x] * q
    lane = iota((1, 128), 1)
    scalars = jnp.where(lane == 64, total_sum(energy), jnp.where(lane == 65, total_sum(curve), 0.0))
    (row,) = row_sums([parts])
    send = jnp.concatenate(
        [
            jnp.where(lane < ND, row, e_ref[0:1]),
            jnp.where(lane < ND, e_ref[1:2], e_ref[2:3]),
            jnp.where(lane < ND, e_ref[3:4], scalars),
        ],
        axis=1,
    )
    send_ref[...] = jnp.broadcast_to(send, (NDEV, 384))


def first_scalars(sums_ref):
    totals = jnp.sum(sums_ref[:, 256:384], axis=0, keepdims=True)
    energy = totals[0:1, 64:65]
    curve = totals[0:1, 65:66]
    return energy, curve, energy / curve


def amounts_kernel(sums_ref, matrix_ref, p_ref, q_ref, c_ref, y_ref, v_ref, r_ref, send_ref, piece_ref):
    _, _, alpha = first_scalars(sums_ref)
    piece_ref[...] = sums_ref[:, 0:128]
    even = piece_ref[pl.ds(0, 64, stride=2), :]
    odd = pltpu.roll(piece_ref[pl.ds(1, 64, stride=2), :], 64, 1)
    amounts = coarse_rows(matrix_ref, even, odd)
    (field,) = fields([amounts])
    sums = [jnp.zeros((CY, CZ), F32) for _ in range(3)]
    for x in range(CX):
        lifted = v_ref[x] * plane_field(field, x // 2)
        p, q, c = p_ref[x], q_ref[x], c_ref[x]
        residual = r_ref[x] - alpha * q
        smooth = p - alpha * c
        smooth_image = q - alpha * y_ref[x]
        precond = smooth - alpha * lifted
        sums[0] = sums[0] + residual * precond
        sums[1] = sums[1] + precond * q
        sums[2] = sums[2] + smooth_image * (smooth - 2.0 * alpha * lifted)
    lane = iota((1, 128), 1)
    row = jnp.where(lane < ND, amounts, 0.0)
    for n in range(3):
        row = jnp.where(lane == ND + n, total_sum(sums[n]), row)
    send_ref[...] = jnp.broadcast_to(row, (NDEV, 128))


def final_kernel(
    pos, sums_ref, got_ref, p_ref, q_ref, c_ref, y_ref, r_ref, vx_ref, w_ref, diag_ref,
    pressure_ref, residual_ref,
    lift_ref, plane_ref,
):
    energy, curve, alpha = first_scalars(sums_ref)
    got = got_ref[...]
    dup = twice(got, 0)
    half = twice(sums_ref[:, 0:128], 1) * dup
    towards = (twice(sums_ref[:, 128:256], 0), twice(sums_ref[:, 128:256], 1), twice(sums_ref[:, 256:384], 0))
    for step in range(3):
        half = half + 2.0 * towards[step] * ahead_behind(dup, step, 1)
    quad = total_sum(jnp.where(iota((NDEV, 128), 1) < ND, half * dup, 0.0))
    totals = jnp.sum(got, axis=0, keepdims=True)
    energy_next = totals[0:1, 64:65]
    mixed = totals[0:1, 65:66]
    beta = energy_next / energy
    curve_next = totals[0:1, 66:67] + alpha * alpha * quad + 2.0 * beta * mixed + beta * beta * curve
    alpha_next = energy_next / curve_next

    me = (pos[0] * 4 + pos[1]) * 8 + pos[2]
    rows = []
    for shift in (0, -32, 32, -8, 8, -1, 1):
        at = jnp.clip(me + shift, 0, NDEV - 1)
        rows.append(got_ref[pl.ds(at, 1), :])
    mine, xm, xp, ym, yp, zm, zp = fields(rows)
    lanes = iota((PY, CZ), 1)
    zeros = jnp.zeros((HY, CZ), F32)
    for i in range(N_V):
        x = i - H_V
        if x < 0 or x >= CX:
            own = plane_field(xm, 3) if x < 0 else plane_field(xp, 0)
            middle = jnp.concatenate([zeros, own, zeros], axis=0)
            side = jnp.zeros((PY, CZ), F32)
        else:
            s = x // 2
            down = jnp.broadcast_to(ym[4 * s + 3 : 4 * s + 4], (HY, CZ))
            up = jnp.broadcast_to(yp[4 * s : 4 * s + 1], (HY, CZ))
            middle = jnp.concatenate([down, plane_field(mine, s), up], axis=0)
            ahead = jnp.concatenate([zeros, plane_field(zp, s), zeros], axis=0)
            behind = jnp.concatenate([zeros, plane_field(zm, s), zeros], axis=0)
            side = jnp.where(lanes < 8, ahead, jnp.where(lanes >= CZ - 8, behind, 0.0))
        lift_ref[0, i] = vx_ref[0, i] * middle
        lift_ref[1, i] = vx_ref[1, i] * side
    for x in range(CX):
        for j in range(ROWS):
            values = around_strided(lambda i, j: strided(lift_ref, i, j), x + H_V, j)
            mine = strided(lift_ref, x + H_V, j)
            total = w_ref[0, x + HX, j] * (mine - values[0])
            for d in range(1, 6):
                total = total + w_ref[d, x + HX, j] * (mine - values[d])
            plane_ref[x, pl.ds(j, 8, stride=ROWS), :] = total[:, 0:CZ] * diag_ref[x, j]
        lifted_image = plane_ref[x, HY : HY + CY]
        lifted = lift_ref[0, x + H_V, HY : HY + CY]
        p, q = p_ref[x], q_ref[x]
        precond = p - alpha * (c_ref[x] + lifted)
        precond_image = q - alpha * (y_ref[x] + lifted_image)
        direction = precond + beta * p
        image = precond_image + beta * q
        pressure_ref[x] = alpha * p + alpha_next * direction
        residual_ref[x] = (r_ref[x] - alpha * q) - alpha_next * image


VMEM = pl.BlockSpec(memory_space=pltpu.VMEM)
SMEM = pl.BlockSpec(memory_space=pltpu.SMEM)


def call(kernel, outs, scratch=(), smem=False, hbm=0, mib=20, cost=None):
    def run(*args):
        many = isinstance(outs, list)
        specs = [VMEM] * len(args)
        if smem:
            specs[0] = SMEM
        for n in range(int(smem), int(smem) + hbm):
            specs[n] = pl.BlockSpec(memory_space=pltpu.HBM)
        return pl.pallas_call(
            kernel,
            out_shape=[jax.ShapeDtypeStruct(s, F32) for s in outs] if many else jax.ShapeDtypeStruct(outs, F32),
            in_specs=specs,
            out_specs=[VMEM] * len(outs) if many else VMEM,
            scratch_shapes=[pltpu.VMEM(s, F32) if isinstance(s, tuple) else s for s in scratch],
            compiler_params=pltpu.CompilerParams(vmem_limit_bytes=mib * 1024 * 1024),
            cost_estimate=cost,
        )(*args)

    return run


def cost(us):
    return pl.CostEstimate(flops=int(us * 1e6), bytes_accessed=int(us * 3e6), transcendentals=0)


def swap(a, b, axis):
    count = lax.axis_size(axis)
    got_a = lax.ppermute(a, axis, [(i, i ^ 1) for i in range(count)])
    got_b = lax.ppermute(b, axis, [(i, (i - 1 if i % 2 == 0 else i + 1) % count) for i in range(count)])
    return got_a, got_b


def gather(rows):
    return lax.all_to_all(rows, AXES, 0, 0, tiled=True)


def exchange_yz(pos, own, count):
    groups = -(-count // 16)
    ya, yb = call(y_kernel, [(count, HY, CZ)] * 2, smem=True)(pos, *own)
    ya, yb = swap(ya, yb, "gy")
    left, right = call(z_own_kernel, [(groups, CY, CZ)] * 2, smem=True, cost=cost(1))(pos, *own)
    za, zb = call(z_kernel, [(groups, PY, CZ)] * 2, smem=True)(pos, ya, yb, left, right)
    return (ya, yb, *swap(za, zb, "gz"))


def local(right_side, phase, deflation_weights, coarse_inverse):
    pos = jnp.stack([lax.axis_index(a) for a in AXES]).astype(jnp.int32)
    block = (CX, CY, CZ)
    tall = (2, PX, PY, CZ)
    split = (PX, ROWS, 8, PZ)
    n_x = H_R + H_G + H_V
    xa, xb, send, r, g, v = call(
        start_kernel,
        [(n_x, CY, CZ), (n_x, CY, CZ), (NDEV, 128), block, block, block],
        scratch=[pltpu.VMEM(block, jnp.int32), pltpu.SemaphoreType.DMA((3,))],
        smem=True,
        hbm=3,
    )(pos, right_side, phase, deflation_weights)
    xa, xb = swap(xa, xb, "gx")
    sums = gather(send)
    xa, xb, sums = lax.optimization_barrier((xa, xb, sums))
    own = (r, g, v, xa, xb)
    halos = exchange_yz(pos, own, N_ALL)
    amounts = call(first_amounts_kernel, (1, 128), cost=cost(1))(sums, coarse_inverse)
    p, xa, xb, v_wide, w, diag = call(
        smooth_kernel,
        [block, (HX, CY, CZ), (HX, CY, CZ), (2, N_V, PY, CZ), (6, *split), (CX, ROWS, 8, CZ)],
        scratch=[tall, (2, N_R, PY, CZ), split, split, split, (CX, PY, CZ)],
        smem=True,
    )(pos, *own, *halos, amounts)
    own = (p, *swap(xa, xb, "gx"))
    quads = call(product_kernel, (4, 128), scratch=[(16, PY, CZ)], cost=cost(1))(v_wide, w, diag)
    halos = exchange_yz(pos, own, PX)
    q, c, y, send = call(
        image_kernel,
        [block, block, block, (NDEV, 384)],
        scratch=[tall, (3 * CX, PY, CZ), split, split, split],
        smem=True,
    )(pos, *own, *halos, w, diag, r, v, quads)
    sums = gather(send)
    send = call(amounts_kernel, (NDEV, 128), scratch=[(NDEV, 128)])(sums, coarse_inverse, p, q, c, y, v, r)
    got = gather(send)
    pressure, residual = call(
        final_kernel, [block, block], scratch=[(2, N_V, PY, CZ), (CX, PY, CZ)], smem=True
    )(pos, sums, got, p, q, c, y, r, v_wide, w, diag)
    return (pressure, residual)


def solution(mesh):
    return jax.shard_map(
        local,
        mesh=mesh,
        in_specs=(P(*AXES), P(*AXES), P(*AXES), P(AXES, None)),
        out_specs=(P(*AXES), P(*AXES)),
        check_vma=False,
    )
```

```python
import functools

import jax
import jax.numpy as jnp
import numpy as np
from jax import lax
from jax.experimental import pallas as pl
from jax.experimental.pallas import tpu as pltpu
from jax.sharding import PartitionSpec as P

AXES = ("gx", "gy", "gz")
SBX = 4
ND = 64
DEG = 6
spectrum_low = 0.08
spectrum_high = 2.0

CX, CY, CZ = 8, 64, 128
HX, HY = 7, 8
PX, PY, PZ = CX + 2 * HX, CY + 2 * HY, 2 * CZ
H_R, H_G, H_V = 5, 7, 1
N_R, N_G, N_V = CX + 2 * H_R, CX + 2 * H_G, CX + 2 * H_V
N_ALL = N_R + N_G + N_V
NDEV = 128
ROWS = PY // 8

LIQUID = np.float32(1.0)
GAS = np.float32(0.001)
F_LL = np.float32(2.0) / (LIQUID + LIQUID)
F_LG = np.float32(2.0) / (LIQUID + GAS)
F_GG = np.float32(2.0) / (GAS + GAS)

def strips(widths):
    room, places = [], {}
    for k, width in sorted(enumerate(widths), key=lambda item: -item[1]):
        if width <= 0:
            continue
        at = next((n for n, free in enumerate(room) if free >= width), len(room))
        if at == len(room):
            room.append(8)
        places[k] = (at, 8 - room[at], width)
        room[at] -= width
    return places, len(room)


def reach(halo, extent):
    return [extent - max(0, -rel, rel - CX + 1) for rel in range(-halo, CX + halo)]


PLACES_1 = strips(reach(H_R, H_R) + reach(H_G, H_G) + reach(H_V, H_V))
PLACES_2 = strips(reach(HX, HX))

F32 = jnp.float32
EXACT = lax.Precision.HIGHEST


def recurrence():
    center = 0.5 * (spectrum_high + spectrum_low)
    half_width = 0.5 * (spectrum_high - spectrum_low)
    ratio = center / half_width
    earlier = 1.0 / ratio
    weights = []
    for index in range(DEG - 1):
        later = 1.0 / (2.0 * ratio - earlier)
        weights.append((later * earlier, 2.0 * later / half_width))
        earlier = later
    return (1.0 / center, weights)


def iota(shape, dim):
    return lax.broadcasted_iota(jnp.int32, shape, dim)


def whole(ref, i):
    return jnp.concatenate([ref[0, i], ref[1, i]], axis=1)


def put(ref, i, plane):
    ref[0, i] = plane[:, 0:CZ]
    ref[1, i] = plane[:, CZ:PZ]


def neighbours(ref, i):
    v = whole(ref, i)
    return (
        whole(ref, i - 1),
        whole(ref, i + 1),
        pltpu.roll(v, 1, 0),
        pltpu.roll(v, PY - 1, 0),
        pltpu.roll(v, 1, 1),
        pltpu.roll(v, PZ - 1, 1),
    )


def strided(ref, i, j):
    rows = pl.ds(j, 8, stride=ROWS)
    return jnp.concatenate([ref[0, i, rows, :], ref[1, i, rows, :]], axis=1)


def around_strided(load, i, j):
    v = load(i, j)
    return (
        load(i - 1, j),
        load(i + 1, j),
        load(i, j - 1) if j else pltpu.roll(load(i, ROWS - 1), 1, 0),
        load(i, j + 1) if j < ROWS - 1 else pltpu.roll(load(i, 0), 7, 0),
        pltpu.roll(v, 1, 1),
        pltpu.roll(v, PZ - 1, 1),
    )


def inside_yz(pos, j=None):
    gy, gz = pos[1], pos[2]
    shape = (PY, PZ) if j is None else (8, PZ)
    row = iota(shape, 0) if j is None else iota(shape, 0) * ROWS + j
    row = row - HY + gy * CY
    lane = iota(shape, 1)
    near = jnp.where(lane < CZ + CZ // 2, lane, lane - PZ) + gz * CZ
    kept = (lane < CZ + 8) | (lane >= PZ - 8)
    good = (row >= 0) & (row < 4 * CY) & (near >= 0) & (near < 8 * CZ) & kept
    return jnp.where(good, 1.0, 0.0).astype(F32)


def inside_x(pos, rel):
    x = pos[0] * CX + rel
    return jnp.where((x >= 0) & (x < 4 * CX), 1.0, 0.0).astype(F32)


def pair(labels):
    gas = labels > 0.5
    return jnp.where(gas, F_LG, F_LL), jnp.where(gas, F_GG - F_LG, F_LG - F_LL)


def row_sums(arrays):
    rows = []
    for parts in arrays:
        for part in parts:
            for sy in range(4):
                rows.append(jnp.sum(part[16 * sy : 16 * sy + 16], axis=0, keepdims=True))
    stacked = jnp.concatenate(rows, axis=0)
    pick = jnp.where(iota((128, 128), 0) // 32 == iota((128, 128), 1) % 4, 1.0, 0.0).astype(F32)
    spread = jnp.dot(stacked, pick, precision=EXACT, preferred_element_type=F32)
    keep = (iota((16, 128), 1) // 4) % 16 == iota((16, 128), 0)
    return [
        jnp.sum(jnp.where(keep, spread[16 * n : 16 * n + 16], 0.0), axis=0, keepdims=True) for n in range(len(arrays))
    ]


def fields(rows):
    count = len(rows)
    keep = (iota((16, 128), 1) // 4 == iota((16, 128), 0)) & (iota((16, 128), 1) < ND)
    tall = jnp.concatenate([jnp.where(keep, jnp.broadcast_to(r, (16, 128)), 0.0) for r in rows], axis=0)
    pick = jnp.where(iota((128, 128), 0) % 4 == iota((128, 128), 1) // 32, 1.0, 0.0).astype(F32)
    out = jnp.dot(tall, pick, precision=EXACT, preferred_element_type=F32)
    return [out[16 * k : 16 * k + 16] for k in range(count)]


def plane_field(field, sx):
    return jnp.concatenate(
        [jnp.broadcast_to(field[4 * sx + sy : 4 * sx + sy + 1], (16, 128)) for sy in range(4)], axis=0
    )


def coarse_rows(matrix_ref, even, odd):
    wide = jnp.where(iota((64, 128), 1) < ND, even, odd)
    total = matrix_ref[:, 0:128] * wide[0:1]
    for t in range(1, 64):
        total = total + matrix_ref[:, 128 * t : 128 * t + 128] * wide[t : t + 1]
    column = jnp.sum(total, axis=1, keepdims=True)
    keep = iota((64, 128), 1) % ND == iota((64, 128), 0)
    return jnp.sum(jnp.where(keep, column, 0.0), axis=0, keepdims=True)


def total_sum(x):
    return jnp.sum(jnp.sum(x, axis=0, keepdims=True), axis=1, keepdims=True)


def start_kernel(pos, r_in, phase_in, v_in, xa_ref, xb_ref, send_ref, r_ref, g_ref, v_ref, phase_ref, sem):
    pairs = ((r_in, r_ref), (v_in, v_ref), (phase_in, phase_ref))
    copies = [pltpu.make_async_copy(src, dst, sem.at[n]) for n, (src, dst) in enumerate(pairs)]
    for copy in copies:
        copy.start()
    for copy in copies:
        copy.wait()
    parts = []
    for sx in range(4):
        parts.append(r_ref[2 * sx] * v_ref[2 * sx] + r_ref[2 * sx + 1] * v_ref[2 * sx + 1])
    (row,) = row_sums([parts])
    send_ref[...] = jnp.broadcast_to(row, (NDEV, 128))
    g_ref[...] = jnp.where(phase_ref[...] == 1, 1.0, 0.0).astype(F32)
    even = is_even(pos, 0)
    for base, ref, halo in ((0, r_ref, H_R), (H_R, g_ref, H_G), (H_R + H_G, v_ref, H_V)):
        for k in range(halo):
            put_pair(even, xa_ref, xb_ref, base + k, ref[k], ref[CX - halo + k])


def is_even(pos, axis):
    return (pos[axis] & 1) == 0


def put_pair(even, a_ref, b_ref, k, down, up):
    a_ref[k] = jnp.where(even, up, down)
    b_ref[k] = jnp.where(even, down, up)


class Pair:
    def __init__(self, pos, axis, a_ref, b_ref):
        self.even, self.a, self.b = is_even(pos, axis), a_ref, b_ref

    def below(self, *at):
        return jnp.where(self.even, self.b[at], self.a[at])

    def above(self, *at):
        return jnp.where(self.even, self.a[at], self.b[at])


def stacked_planes(r_ref, g_ref, v_ref, sides):
    planes = []
    for halo, ref, base in ((H_R, r_ref, 0), (H_G, g_ref, H_R), (H_V, v_ref, H_R + H_G)):
        for rel in range(-halo, CX + halo):
            if rel < 0:
                planes.append(lambda s, k=base + rel + halo: sides.below(k, s))
            elif rel >= CX:
                planes.append(lambda s, k=base + rel - CX: sides.above(k, s))
            else:
                planes.append(lambda s, k=rel, ref=ref: ref[k, s])
    return planes


def padded_planes(p_ref, sides):
    planes = []
    for rel in range(-HX, CX + HX):
        if rel < 0:
            planes.append(lambda s, k=rel + HX: sides.below(k, s))
        elif rel >= CX:
            planes.append(lambda s, k=rel - CX: sides.above(k, s))
        else:
            planes.append(lambda s, k=rel: p_ref[k, s])
    return planes


def all_planes(refs, pos):
    sides = Pair(pos, 0, *refs[-2:])
    return padded_planes(refs[0], sides) if len(refs) == 3 else stacked_planes(*refs[:3], sides)


def places_of(refs):
    return PLACES_2[0] if len(refs) == 3 else PLACES_1[0]


def turn(x, shift, axis):
    shift %= x.shape[axis]
    return pltpu.roll(x, shift, axis) if shift else x


def y_kernel(pos, *refs):
    refs, (a_ref, b_ref) = refs[:-2], refs[-2:]
    even = is_even(pos, 1)
    planes = all_planes(refs, pos)
    row = iota((HY, CZ), 0)
    tiles = {}
    for k, (at, off, width) in places_of(refs).items():
        down, up = tiles.get(at, (jnp.zeros((HY, CZ), F32),) * 2)
        here = (row >= off) & (row < off + width)
        down = jnp.where(here, turn(planes[k](pl.ds(0, HY)), off, 0), down)
        up = jnp.where(here, turn(planes[k](pl.ds(CY - HY, HY)), off + width, 0), up)
        tiles[at] = (down, up)
    for at, (down, up) in tiles.items():
        put_pair(even, a_ref, b_ref, at, down, up)


def pack_lanes(value, places, rows):
    lane = iota((rows, CZ), 1)
    packed = {}
    for k, (at, off, width) in places.items():
        group, start = at // 16, at % 16 * 8 + off
        left, right = packed.get(group, (jnp.zeros((rows, CZ), F32),) * 2)
        here = (lane >= start) & (lane < start + width)
        left = jnp.where(here, turn(value(k), start, 1), left)
        right = jnp.where(here, turn(value(k), start + width, 1), right)
        packed[group] = (left, right)
    return packed


def z_own_kernel(pos, *refs):
    refs, (left_ref, right_ref) = refs[:-2], refs[-2:]
    planes = all_planes(refs, pos)
    for group, (left, right) in pack_lanes(lambda k: planes[k](pl.ds(0, CY)), places_of(refs), CY).items():
        left_ref[group] = left
        right_ref[group] = right


class Rows:
    def __init__(self, pos, places, a_ref, b_ref):
        self.pair, self.places = Pair(pos, 1, a_ref, b_ref), places

    def below(self, k):
        if k not in self.places:
            return jnp.zeros((HY, CZ), F32)
        at, off, width = self.places[k]
        return turn(self.pair.below(at), -off - width, 0)

    def above(self, k):
        if k not in self.places:
            return jnp.zeros((HY, CZ), F32)
        at, off, _ = self.places[k]
        return turn(self.pair.above(at), -off, 0)


def z_kernel(places, pos, ya_ref, yb_ref, left_ref, right_ref, za_ref, zb_ref):
    even = is_even(pos, 2)
    rows = Rows(pos, places, ya_ref, yb_ref)
    below = pack_lanes(rows.below, places, HY)
    above = pack_lanes(rows.above, places, HY)
    for group in below:
        left = jnp.concatenate([below[group][0], left_ref[group], above[group][0]], axis=0)
        right = jnp.concatenate([below[group][1], right_ref[group], above[group][1]], axis=0)
        put_pair(even, za_ref, zb_ref, group, left, right)


class Wide:
    def __init__(self, planes, places, pos, ya_ref, yb_ref, za_ref, zb_ref):
        self.planes, self.places = planes, places
        self.rows = Rows(pos, places, ya_ref, yb_ref)
        z = Pair(pos, 2, za_ref, zb_ref)
        groups = za_ref.shape[0]
        self.behind = [z.below(g) for g in range(groups)]
        self.ahead = [z.above(g) for g in range(groups)]

    def __call__(self, k):
        lane = iota((PY, CZ), 1)
        side = jnp.zeros((PY, CZ), F32)
        if k in self.places:
            at, off, width = self.places[k]
            group, start = at // 16, at % 16 * 8 + off
            ahead = turn(self.ahead[group], -start, 1)
            behind = turn(self.behind[group], -start - width, 1)
            side = jnp.where(lane < 8, ahead, jnp.where(lane >= CZ - 8, behind, 0.0))
        middle = jnp.concatenate([self.rows.below(k), self.planes[k](pl.ds(0, CY)), self.rows.above(k)], axis=0)
        return jnp.concatenate([middle, side], axis=1)


def first_amounts_kernel(sums_ref, matrix_ref, out_ref):
    out_ref[...] = coarse_rows(matrix_ref, sums_ref[pl.ds(0, 64, stride=2), :], sums_ref[pl.ds(1, 64, stride=2), :])


def chebyshev(halo, w_ref, rp_ref, a_ref, b_ref):
    _, weights = recurrence()
    now, before = a_ref, b_ref
    for index, (keep, push) in enumerate(weights):
        halo -= 1
        for i in range(HX - halo, HX + CX + halo):
            for j in range(ROWS):
                around = around_strided(lambda i, j: now[i, j], i, j)
                total = rp_ref[i, j]
                for d in range(6):
                    total = total + w_ref[d, i, j] * around[d]
                new = (1.0 + keep - push) * now[i, j] + push * total
                if index:
                    new = new - keep * before[i, j]
                before[i, j] = new
        now, before = before, now
    return now


def smooth_kernel(
    pos, r_ref, g_in, v_in, xa_ref, xb_ref, ya_ref, yb_ref, za_ref, zb_ref, amounts_ref,
    p_ref, xa_out, xb_out, vx_ref, w_ref, diag_ref,
    g_ref, wide_ref, rp_ref, a_ref, b_ref, nat_ref,
):
    planes = stacked_planes(r_ref, g_in, v_in, Pair(pos, 0, xa_ref, xb_ref))
    wide = Wide(planes, PLACES_1[0], pos, ya_ref, yb_ref, za_ref, zb_ref)
    mask = inside_yz(pos)
    for i in range(PX):
        put(g_ref, i, jnp.where(wide(N_R + i) > 0.5, mask * inside_x(pos, i - HX), 0.0))
    for i in range(N_V):
        put(vx_ref, i, wide(N_R + N_G + i) * (mask * inside_x(pos, i - H_V)))
    for k in range(N_R):
        put(wide_ref, k, wide(k))
    first_scale, _ = recurrence()
    for j in range(ROWS):
        mask = inside_yz(pos, j)
        for i in range(1, PX - 1):
            labels = around_strided(lambda i, j: strided(g_ref, i, j), i, j)
            first, second = pair(strided(g_ref, i, j))
            count = (labels[0] + labels[1]) + (labels[2] + labels[3]) + (labels[4] + labels[5])
            diagonal = 6.0 * first + second * count
            if HX <= i < HX + CX:
                diag_ref[i - HX, j] = diagonal[:, 0:CZ]
            inverse = mask * inside_x(pos, i - HX) / diagonal
            first, second = first * inverse, second * inverse
            for d in range(6):
                w_ref[d, i, j] = first + second * labels[d]
            if HX - H_R <= i < HX + CX + H_R:
                scaled = strided(wide_ref, i - HX + H_R, j) * inverse
                rp_ref[i, j] = scaled
                a_ref[i, j] = scaled * first_scale
    result = chebyshev(H_R, w_ref, rp_ref, a_ref, b_ref)
    for j in range(ROWS):
        for x in range(CX):
            nat_ref[x, pl.ds(j, 8, stride=ROWS), :] = result[HX + x, j, :, 0:CZ]
    (field,) = fields([amounts_ref[...]])
    for x in range(CX):
        p_ref[x] = nat_ref[x, HY : HY + CY] + v_in[x] * plane_field(field, x // 2)
    even = is_even(pos, 0)
    for k in range(HX):
        put_pair(even, xa_out, xb_out, k, p_ref[k], p_ref[CX - HX + k])


def product_kernel(vx_ref, w_ref, diag_ref, out_ref, acc_ref):
    for j in range(ROWS):
        rows = pl.ds(j, 8, stride=ROWS)
        last_y = (iota((8, CZ), 0) * ROWS + j - HY) % 16 == 15
        last_z = iota((8, CZ), 1) % 32 == 31
        for sx in range(4):
            sums = [jnp.zeros((8, CZ), F32) for _ in range(4)]
            for x in (2 * sx, 2 * sx + 1):
                mine = strided(vx_ref, x + H_V, j)
                ahead = (
                    strided(vx_ref, x + H_V + 1, j),
                    strided(vx_ref, x + H_V, j + 1) if j < ROWS - 1 else pltpu.roll(strided(vx_ref, x + H_V, 0), 7, 0),
                    pltpu.roll(mine, PZ - 1, 1),
                )
                scaled = diag_ref[x, j] * mine[:, 0:CZ]
                cross = [scaled * w_ref[2 * d + 1, x + HX, j, :, 0:CZ] * ahead[d][:, 0:CZ] for d in range(3)]
                inner = jnp.where(last_y, 0.0, cross[1]) + jnp.where(last_z, 0.0, cross[2])
                if x % 2 == 0:
                    inner = inner + cross[0]
                else:
                    sums[1] = sums[1] - cross[0]
                sums[0] = sums[0] + (scaled * mine[:, 0:CZ] - 2.0 * inner)
                sums[2] = sums[2] - jnp.where(last_y, cross[1], 0.0)
                sums[3] = sums[3] - jnp.where(last_z, cross[2], 0.0)
            for n in range(4):
                acc_ref[4 * n + sx, rows, :] = sums[n]
    quads = row_sums([[acc_ref[4 * n + sx, HY : HY + CY] for sx in range(4)] for n in range(4)])
    for n in range(4):
        out_ref[n : n + 1] = quads[n]


def image_of(ref, w_ref, diag_ref, x, j):
    values = around_strided(lambda i, j: ref[i, j], x + HX, j)
    mine = ref[x + HX, j]
    total = w_ref[0, x + HX, j] * (mine - values[0])
    for d in range(1, 6):
        total = total + w_ref[d, x + HX, j] * (mine - values[d])
    return mine[:, 0:CZ], total[:, 0:CZ] * diag_ref[x, j]


def twice(x, half):
    lane = iota(x.shape, 1)
    other = pltpu.roll(x, ND, 1)
    return jnp.where(lane < ND, x, other) if half == 0 else jnp.where(lane < ND, other, x)


def ahead_behind(x, step, sign):
    lane = iota(x.shape, 1)
    stride, devices = ((16, 32), (4, 8), (1, 1))[step]
    place = (lane // stride) % 4
    near = pltpu.roll(x, (128 - stride * sign) % 128, 1)
    far = pltpu.roll(x, (3 * stride * sign) % 128, 1)
    far = pltpu.roll(far, (NDEV - devices * sign) % NDEV, 0)
    return jnp.where(place != (3 if sign > 0 else 0), near, far)


def image_kernel(
    pos, p_ref, xa_ref, xb_ref, ya_ref, yb_ref, za_ref, zb_ref, w_ref, diag_ref, r_ref, v_ref, e_ref,
    q_ref, c_ref, y_ref, send_ref,
    full_ref, plane_ref, rp_ref, a_ref, b_ref,
):
    planes = padded_planes(p_ref, Pair(pos, 0, xa_ref, xb_ref))
    wide = Wide(planes, PLACES_2[0], pos, ya_ref, yb_ref, za_ref, zb_ref)
    mask = inside_yz(pos)
    for i in range(PX):
        put(full_ref, i, wide(i) * (mask * inside_x(pos, i - HX)))
    first_scale, _ = recurrence()
    for j in range(ROWS):
        rows = pl.ds(j, 8, stride=ROWS)
        for i in range(1, PX - 1):
            values = around_strided(lambda i, j: strided(full_ref, i, j), i, j)
            mine = strided(full_ref, i, j)
            total = w_ref[0, i, j] * (mine - values[0])
            for d in range(1, 6):
                total = total + w_ref[d, i, j] * (mine - values[d])
            rp_ref[i, j] = total
            a_ref[i, j] = total * first_scale
            if HX <= i < HX + CX:
                plane_ref[i - HX, rows, :] = total[:, 0:CZ] * diag_ref[i - HX, j]
    result = chebyshev(HX - 1, w_ref, rp_ref, a_ref, b_ref)
    for x in range(CX):
        for j in range(ROWS):
            rows = pl.ds(j, 8, stride=ROWS)
            mine, image = image_of(result, w_ref, diag_ref, x, j)
            plane_ref[CX + x, rows, :] = mine
            plane_ref[2 * CX + x, rows, :] = image
    parts = [jnp.zeros((CY, CZ), F32) for _ in range(4)]
    energy = jnp.zeros((CY, CZ), F32)
    curve = jnp.zeros((CY, CZ), F32)
    for x in range(CX):
        q, c, y = (plane_ref[CX * n + x, HY : HY + CY] for n in range(3))
        q_ref[x], c_ref[x], y_ref[x] = q, c, y
        energy = energy + r_ref[x] * p_ref[x]
        curve = curve + q * p_ref[x]
        parts[x // 2] = parts[x // 2] + v_ref[x] * q
    lane = iota((1, 128), 1)
    scalars = jnp.where(lane == 64, total_sum(energy), jnp.where(lane == 65, total_sum(curve), 0.0))
    (row,) = row_sums([parts])
    send = jnp.concatenate(
        [
            jnp.where(lane < ND, row, e_ref[0:1]),
            jnp.where(lane < ND, e_ref[1:2], e_ref[2:3]),
            jnp.where(lane < ND, e_ref[3:4], scalars),
        ],
        axis=1,
    )
    send_ref[...] = jnp.broadcast_to(send, (NDEV, 384))


def first_scalars(sums_ref):
    totals = jnp.sum(sums_ref[:, 256:384], axis=0, keepdims=True)
    energy = totals[0:1, 64:65]
    curve = totals[0:1, 65:66]
    return energy, curve, energy / curve


def amounts_kernel(sums_ref, matrix_ref, p_ref, q_ref, c_ref, y_ref, v_ref, r_ref, send_ref, piece_ref):
    _, _, alpha = first_scalars(sums_ref)
    piece_ref[...] = sums_ref[:, 0:128]
    even = piece_ref[pl.ds(0, 64, stride=2), :]
    odd = pltpu.roll(piece_ref[pl.ds(1, 64, stride=2), :], 64, 1)
    amounts = coarse_rows(matrix_ref, even, odd)
    (field,) = fields([amounts])
    sums = [jnp.zeros((CY, CZ), F32) for _ in range(3)]
    for x in range(CX):
        lifted = v_ref[x] * plane_field(field, x // 2)
        p, q, c = p_ref[x], q_ref[x], c_ref[x]
        residual = r_ref[x] - alpha * q
        smooth = p - alpha * c
        smooth_image = q - alpha * y_ref[x]
        precond = smooth - alpha * lifted
        sums[0] = sums[0] + residual * precond
        sums[1] = sums[1] + precond * q
        sums[2] = sums[2] + smooth_image * (smooth - 2.0 * alpha * lifted)
    lane = iota((1, 128), 1)
    row = jnp.where(lane < ND, amounts, 0.0)
    for n in range(3):
        row = jnp.where(lane == ND + n, total_sum(sums[n]), row)
    send_ref[...] = jnp.broadcast_to(row, (NDEV, 128))


def final_kernel(
    pos, sums_ref, got_ref, p_ref, q_ref, c_ref, y_ref, r_ref, vx_ref, w_ref, diag_ref,
    pressure_ref, residual_ref,
    lift_ref, plane_ref,
):
    energy, curve, alpha = first_scalars(sums_ref)
    got = got_ref[...]
    dup = twice(got, 0)
    half = twice(sums_ref[:, 0:128], 1) * dup
    towards = (twice(sums_ref[:, 128:256], 0), twice(sums_ref[:, 128:256], 1), twice(sums_ref[:, 256:384], 0))
    for step in range(3):
        half = half + 2.0 * towards[step] * ahead_behind(dup, step, 1)
    quad = total_sum(jnp.where(iota((NDEV, 128), 1) < ND, half * dup, 0.0))
    totals = jnp.sum(got, axis=0, keepdims=True)
    energy_next = totals[0:1, 64:65]
    mixed = totals[0:1, 65:66]
    beta = energy_next / energy
    curve_next = totals[0:1, 66:67] + alpha * alpha * quad + 2.0 * beta * mixed + beta * beta * curve
    alpha_next = energy_next / curve_next

    me = (pos[0] * 4 + pos[1]) * 8 + pos[2]
    rows = []
    for shift in (0, -32, 32, -8, 8, -1, 1):
        at = jnp.clip(me + shift, 0, NDEV - 1)
        rows.append(got_ref[pl.ds(at, 1), :])
    mine, xm, xp, ym, yp, zm, zp = fields(rows)
    lanes = iota((PY, CZ), 1)
    zeros = jnp.zeros((HY, CZ), F32)
    for i in range(N_V):
        x = i - H_V
        if x < 0 or x >= CX:
            own = plane_field(xm, 3) if x < 0 else plane_field(xp, 0)
            middle = jnp.concatenate([zeros, own, zeros], axis=0)
            side = jnp.zeros((PY, CZ), F32)
        else:
            s = x // 2
            down = jnp.broadcast_to(ym[4 * s + 3 : 4 * s + 4], (HY, CZ))
            up = jnp.broadcast_to(yp[4 * s : 4 * s + 1], (HY, CZ))
            middle = jnp.concatenate([down, plane_field(mine, s), up], axis=0)
            ahead = jnp.concatenate([zeros, plane_field(zp, s), zeros], axis=0)
            behind = jnp.concatenate([zeros, plane_field(zm, s), zeros], axis=0)
            side = jnp.where(lanes < 8, ahead, jnp.where(lanes >= CZ - 8, behind, 0.0))
        lift_ref[0, i] = vx_ref[0, i] * middle
        lift_ref[1, i] = vx_ref[1, i] * side
    for x in range(CX):
        for j in range(ROWS):
            values = around_strided(lambda i, j: strided(lift_ref, i, j), x + H_V, j)
            mine = strided(lift_ref, x + H_V, j)
            total = w_ref[0, x + HX, j] * (mine - values[0])
            for d in range(1, 6):
                total = total + w_ref[d, x + HX, j] * (mine - values[d])
            plane_ref[x, pl.ds(j, 8, stride=ROWS), :] = total[:, 0:CZ] * diag_ref[x, j]
        lifted_image = plane_ref[x, HY : HY + CY]
        lifted = lift_ref[0, x + H_V, HY : HY + CY]
        p, q = p_ref[x], q_ref[x]
        precond = p - alpha * (c_ref[x] + lifted)
        precond_image = q - alpha * (y_ref[x] + lifted_image)
        direction = precond + beta * p
        image = precond_image + beta * q
        pressure_ref[x] = alpha * p + alpha_next * direction
        residual_ref[x] = (r_ref[x] - alpha * q) - alpha_next * image


VMEM = pl.BlockSpec(memory_space=pltpu.VMEM)
SMEM = pl.BlockSpec(memory_space=pltpu.SMEM)


def call(kernel, outs, scratch=(), smem=False, hbm=0, mib=20, cost=None):
    def run(*args):
        many = isinstance(outs, list)
        specs = [VMEM] * len(args)
        if smem:
            specs[0] = SMEM
        for n in range(int(smem), int(smem) + hbm):
            specs[n] = pl.BlockSpec(memory_space=pltpu.HBM)
        return pl.pallas_call(
            kernel,
            out_shape=[jax.ShapeDtypeStruct(s, F32) for s in outs] if many else jax.ShapeDtypeStruct(outs, F32),
            in_specs=specs,
            out_specs=[VMEM] * len(outs) if many else VMEM,
            scratch_shapes=[pltpu.VMEM(s, F32) if isinstance(s, tuple) else s for s in scratch],
            compiler_params=pltpu.CompilerParams(vmem_limit_bytes=mib * 1024 * 1024),
            cost_estimate=cost,
        )(*args)

    return run


def cost(us):
    return pl.CostEstimate(flops=int(us * 1e6), bytes_accessed=int(us * 3e6), transcendentals=0)


def swap(a, b, axis):
    count = lax.axis_size(axis)
    got_a = lax.ppermute(a, axis, [(i, i ^ 1) for i in range(count)])
    got_b = lax.ppermute(b, axis, [(i, (i - 1 if i % 2 == 0 else i + 1) % count) for i in range(count)])
    return got_a, got_b


def gather(rows):
    return lax.all_to_all(rows, AXES, 0, 0, tiled=True)


def exchange_yz(pos, own):
    places, count = PLACES_2 if len(own) == 3 else PLACES_1
    groups = -(-count // 16)
    ya, yb = call(y_kernel, [(count, HY, CZ)] * 2, smem=True)(pos, *own)
    ya, yb = swap(ya, yb, "gy")
    left, right = call(z_own_kernel, [(groups, CY, CZ)] * 2, smem=True, cost=cost(1))(pos, *own)
    pack = functools.partial(z_kernel, places)
    za, zb = call(pack, [(groups, PY, CZ)] * 2, smem=True)(pos, ya, yb, left, right)
    return (ya, yb, *swap(za, zb, "gz"))


def local(right_side, phase, deflation_weights, coarse_inverse):
    pos = jnp.stack([lax.axis_index(a) for a in AXES]).astype(jnp.int32)
    block = (CX, CY, CZ)
    tall = (2, PX, PY, CZ)
    split = (PX, ROWS, 8, PZ)
    n_x = H_R + H_G + H_V
    xa, xb, send, r, g, v = call(
        start_kernel,
        [(n_x, CY, CZ), (n_x, CY, CZ), (NDEV, 128), block, block, block],
        scratch=[pltpu.VMEM(block, jnp.int32), pltpu.SemaphoreType.DMA((3,))],
        smem=True,
        hbm=3,
    )(pos, right_side, phase, deflation_weights)
    xa, xb = swap(xa, xb, "gx")
    sums = gather(send)
    xa, xb, sums = lax.optimization_barrier((xa, xb, sums))
    own = (r, g, v, xa, xb)
    halos = exchange_yz(pos, own)
    amounts = call(first_amounts_kernel, (1, 128), cost=cost(1))(sums, coarse_inverse)
    p, xa, xb, v_wide, w, diag = call(
        smooth_kernel,
        [block, (HX, CY, CZ), (HX, CY, CZ), (2, N_V, PY, CZ), (6, *split), (CX, ROWS, 8, CZ)],
        scratch=[tall, (2, N_R, PY, CZ), split, split, split, (CX, PY, CZ)],
        smem=True,
    )(pos, *own, *halos, amounts)
    own = (p, *swap(xa, xb, "gx"))
    quads = call(product_kernel, (4, 128), scratch=[(16, PY, CZ)], cost=cost(1))(v_wide, w, diag)
    halos = exchange_yz(pos, own)
    q, c, y, send = call(
        image_kernel,
        [block, block, block, (NDEV, 384)],
        scratch=[tall, (3 * CX, PY, CZ), split, split, split],
        smem=True,
    )(pos, *own, *halos, w, diag, r, v, quads)
    sums = gather(send)
    send = call(amounts_kernel, (NDEV, 128), scratch=[(NDEV, 128)])(sums, coarse_inverse, p, q, c, y, v, r)
    got = gather(send)
    pressure, residual = call(
        final_kernel, [block, block], scratch=[(2, N_V, PY, CZ), (CX, PY, CZ)], smem=True
    )(pos, sums, got, p, q, c, y, r, v_wide, w, diag)
    return (pressure, residual)


def solution(mesh):
    return jax.shard_map(
        local,
        mesh=mesh,
        in_specs=(P(*AXES), P(*AXES), P(*AXES), P(AXES, None)),
        out_specs=(P(*AXES), P(*AXES)),
        check_vma=False,
    )
```

```python
import functools

import jax
import jax.numpy as jnp
import numpy as np
from jax import lax
from jax.experimental import pallas as pl
from jax.experimental.pallas import tpu as pltpu
from jax.sharding import PartitionSpec as P

AXES = ("gx", "gy", "gz")
SBX = 4
ND = 64
DEG = 6
spectrum_low = 0.08
spectrum_high = 2.0

CX, CY, CZ = 8, 64, 128
HX, HY = 7, 8
PX, PY, PZ = CX + 2 * HX, CY + 2 * HY, 2 * CZ
H_R, H_G, H_V = 5, 7, 1
N_R, N_G, N_V = CX + 2 * H_R, CX + 2 * H_G, CX + 2 * H_V
N_ALL = N_R + N_G + N_V
NDEV = 128
ROWS = PY // 8

LIQUID = np.float32(1.0)
GAS = np.float32(0.001)
F_LL = np.float32(2.0) / (LIQUID + LIQUID)
F_LG = np.float32(2.0) / (LIQUID + GAS)
F_GG = np.float32(2.0) / (GAS + GAS)

def strips(widths):
    room, places = [], {}
    for k, width in sorted(enumerate(widths), key=lambda item: -item[1]):
        if width <= 0:
            continue
        at = next((n for n, free in enumerate(room) if free >= width), len(room))
        if at == len(room):
            room.append(8)
        places[k] = (at, 8 - room[at], width)
        room[at] -= width
    return places, len(room)


def reach(halo, extent):
    return [extent - max(0, -rel, rel - CX + 1) for rel in range(-halo, CX + halo)]


PLACES_1 = strips(reach(H_R, H_R) + reach(H_G, H_G) + reach(H_V, H_V))
PLACES_2 = strips(reach(HX, HX))

F32 = jnp.float32
EXACT = lax.Precision.HIGHEST


def recurrence():
    center = 0.5 * (spectrum_high + spectrum_low)
    half_width = 0.5 * (spectrum_high - spectrum_low)
    ratio = center / half_width
    earlier = 1.0 / ratio
    weights = []
    for index in range(DEG - 1):
        later = 1.0 / (2.0 * ratio - earlier)
        weights.append((later * earlier, 2.0 * later / half_width))
        earlier = later
    return (1.0 / center, weights)


def iota(shape, dim):
    return lax.broadcasted_iota(jnp.int32, shape, dim)


def whole(ref, i):
    return jnp.concatenate([ref[0, i], ref[1, i]], axis=1)


def put(ref, i, plane):
    ref[0, i] = plane[:, 0:CZ]
    ref[1, i] = plane[:, CZ:PZ]


def neighbours(ref, i):
    v = whole(ref, i)
    return (
        whole(ref, i - 1),
        whole(ref, i + 1),
        pltpu.roll(v, 1, 0),
        pltpu.roll(v, PY - 1, 0),
        pltpu.roll(v, 1, 1),
        pltpu.roll(v, PZ - 1, 1),
    )


def strided(ref, i, j):
    rows = pl.ds(j, 8, stride=ROWS)
    return jnp.concatenate([ref[0, i, rows, :], ref[1, i, rows, :]], axis=1)


def around_strided(load, i, j):
    v = load(i, j)
    return (
        load(i - 1, j),
        load(i + 1, j),
        load(i, j - 1) if j else pltpu.roll(load(i, ROWS - 1), 1, 0),
        load(i, j + 1) if j < ROWS - 1 else pltpu.roll(load(i, 0), 7, 0),
        pltpu.roll(v, 1, 1),
        pltpu.roll(v, PZ - 1, 1),
    )


def inside_yz(pos, j=None):
    gy, gz = pos[1], pos[2]
    shape = (PY, PZ) if j is None else (8, PZ)
    row = iota(shape, 0) if j is None else iota(shape, 0) * ROWS + j
    row = row - HY + gy * CY
    lane = iota(shape, 1)
    near = jnp.where(lane < CZ + CZ // 2, lane, lane - PZ) + gz * CZ
    kept = (lane < CZ + 8) | (lane >= PZ - 8)
    good = (row >= 0) & (row < 4 * CY) & (near >= 0) & (near < 8 * CZ) & kept
    return jnp.where(good, 1.0, 0.0).astype(F32)


def inside_x(pos, rel):
    x = pos[0] * CX + rel
    return jnp.where((x >= 0) & (x < 4 * CX), 1.0, 0.0).astype(F32)


def pair(labels):
    gas = labels > 0.5
    return jnp.where(gas, F_LG, F_LL), jnp.where(gas, F_GG - F_LG, F_LG - F_LL)


def row_sums(arrays):
    rows = []
    for parts in arrays:
        for part in parts:
            for sy in range(4):
                rows.append(jnp.sum(part[16 * sy : 16 * sy + 16], axis=0, keepdims=True))
    stacked = jnp.concatenate(rows, axis=0)
    pick = jnp.where(iota((128, 128), 0) // 32 == iota((128, 128), 1) % 4, 1.0, 0.0).astype(F32)
    spread = jnp.dot(stacked, pick, precision=EXACT, preferred_element_type=F32)
    keep = (iota((16, 128), 1) // 4) % 16 == iota((16, 128), 0)
    return [
        jnp.sum(jnp.where(keep, spread[16 * n : 16 * n + 16], 0.0), axis=0, keepdims=True) for n in range(len(arrays))
    ]


def fields(rows):
    count = len(rows)
    keep = (iota((16, 128), 1) // 4 == iota((16, 128), 0)) & (iota((16, 128), 1) < ND)
    tall = jnp.concatenate([jnp.where(keep, jnp.broadcast_to(r, (16, 128)), 0.0) for r in rows], axis=0)
    pick = jnp.where(iota((128, 128), 0) % 4 == iota((128, 128), 1) // 32, 1.0, 0.0).astype(F32)
    out = jnp.dot(tall, pick, precision=EXACT, preferred_element_type=F32)
    return [out[16 * k : 16 * k + 16] for k in range(count)]


def plane_field(field, sx):
    return jnp.concatenate(
        [jnp.broadcast_to(field[4 * sx + sy : 4 * sx + sy + 1], (16, 128)) for sy in range(4)], axis=0
    )


def coarse_rows(matrix_ref, even, odd):
    wide = jnp.where(iota((64, 128), 1) < ND, even, odd)
    total = matrix_ref[:, 0:128] * wide[0:1]
    for t in range(1, 64):
        total = total + matrix_ref[:, 128 * t : 128 * t + 128] * wide[t : t + 1]
    column = jnp.sum(total, axis=1, keepdims=True)
    keep = iota((64, 128), 1) % ND == iota((64, 128), 0)
    return jnp.sum(jnp.where(keep, column, 0.0), axis=0, keepdims=True)


def total_sum(x):
    return jnp.sum(jnp.sum(x, axis=0, keepdims=True), axis=1, keepdims=True)


def start_kernel(pos, all_ref, xa_ref, xb_ref, send_ref, r_ref, g_ref, v_ref):
    r_ref[...] = all_ref[0:CX]
    g_ref[...] = all_ref[CX : 2 * CX]
    v_ref[...] = all_ref[2 * CX :]
    parts = []
    for sx in range(4):
        parts.append(r_ref[2 * sx] * v_ref[2 * sx] + r_ref[2 * sx + 1] * v_ref[2 * sx + 1])
    (row,) = row_sums([parts])
    send_ref[...] = jnp.broadcast_to(row, (NDEV, 128))
    even = is_even(pos, 0)
    for base, ref, halo in ((0, r_ref, H_R), (H_R, g_ref, H_G), (H_R + H_G, v_ref, H_V)):
        for k in range(halo):
            put_pair(even, xa_ref, xb_ref, base + k, ref[k], ref[CX - halo + k])


def is_even(pos, axis):
    return (pos[axis] & 1) == 0


def put_pair(even, a_ref, b_ref, k, down, up):
    a_ref[k] = jnp.where(even, up, down)
    b_ref[k] = jnp.where(even, down, up)


class Pair:
    def __init__(self, pos, axis, a_ref, b_ref):
        self.even, self.a, self.b = is_even(pos, axis), a_ref, b_ref

    def below(self, *at):
        return jnp.where(self.even, self.b[at], self.a[at])

    def above(self, *at):
        return jnp.where(self.even, self.a[at], self.b[at])


def stacked_planes(r_ref, g_ref, v_ref, sides):
    planes = []
    for halo, ref, base in ((H_R, r_ref, 0), (H_G, g_ref, H_R), (H_V, v_ref, H_R + H_G)):
        for rel in range(-halo, CX + halo):
            if rel < 0:
                planes.append(lambda s, k=base + rel + halo: sides.below(k, s))
            elif rel >= CX:
                planes.append(lambda s, k=base + rel - CX: sides.above(k, s))
            else:
                planes.append(lambda s, k=rel, ref=ref: ref[k, s])
    return planes


def padded_planes(p_ref, sides):
    planes = []
    for rel in range(-HX, CX + HX):
        if rel < 0:
            planes.append(lambda s, k=rel + HX: sides.below(k, s))
        elif rel >= CX:
            planes.append(lambda s, k=rel - CX: sides.above(k, s))
        else:
            planes.append(lambda s, k=rel: p_ref[k, s])
    return planes


def all_planes(refs, pos):
    sides = Pair(pos, 0, *refs[-2:])
    return padded_planes(refs[0], sides) if len(refs) == 3 else stacked_planes(*refs[:3], sides)


def places_of(refs):
    return PLACES_2[0] if len(refs) == 3 else PLACES_1[0]


def turn(x, shift, axis):
    shift %= x.shape[axis]
    return pltpu.roll(x, shift, axis) if shift else x


def y_kernel(pos, *refs):
    refs, (a_ref, b_ref) = refs[:-2], refs[-2:]
    even = is_even(pos, 1)
    planes = all_planes(refs, pos)
    row = iota((HY, CZ), 0)
    tiles = {}
    for k, (at, off, width) in places_of(refs).items():
        down, up = tiles.get(at, (jnp.zeros((HY, CZ), F32),) * 2)
        here = (row >= off) & (row < off + width)
        down = jnp.where(here, turn(planes[k](pl.ds(0, HY)), off, 0), down)
        up = jnp.where(here, turn(planes[k](pl.ds(CY - HY, HY)), off + width, 0), up)
        tiles[at] = (down, up)
    for at, (down, up) in tiles.items():
        put_pair(even, a_ref, b_ref, at, down, up)


def pack_lanes(value, places, rows):
    lane = iota((rows, CZ), 1)
    packed = {}
    for k, (at, off, width) in places.items():
        group, start = at // 16, at % 16 * 8 + off
        left, right = packed.get(group, (jnp.zeros((rows, CZ), F32),) * 2)
        here = (lane >= start) & (lane < start + width)
        left = jnp.where(here, turn(value(k), start, 1), left)
        right = jnp.where(here, turn(value(k), start + width, 1), right)
        packed[group] = (left, right)
    return packed


def z_own_kernel(pos, *refs):
    refs, (left_ref, right_ref) = refs[:-2], refs[-2:]
    planes = all_planes(refs, pos)
    for group, (left, right) in pack_lanes(lambda k: planes[k](pl.ds(0, CY)), places_of(refs), CY).items():
        left_ref[group] = left
        right_ref[group] = right


class Rows:
    def __init__(self, pos, places, a_ref, b_ref):
        self.pair, self.places = Pair(pos, 1, a_ref, b_ref), places

    def below(self, k):
        if k not in self.places:
            return jnp.zeros((HY, CZ), F32)
        at, off, width = self.places[k]
        return turn(self.pair.below(at), -off - width, 0)

    def above(self, k):
        if k not in self.places:
            return jnp.zeros((HY, CZ), F32)
        at, off, _ = self.places[k]
        return turn(self.pair.above(at), -off, 0)


def z_kernel(places, pos, ya_ref, yb_ref, left_ref, right_ref, za_ref, zb_ref):
    even = is_even(pos, 2)
    rows = Rows(pos, places, ya_ref, yb_ref)
    below = pack_lanes(rows.below, places, HY)
    above = pack_lanes(rows.above, places, HY)
    for group in below:
        left = jnp.concatenate([below[group][0], left_ref[group], above[group][0]], axis=0)
        right = jnp.concatenate([below[group][1], right_ref[group], above[group][1]], axis=0)
        put_pair(even, za_ref, zb_ref, group, left, right)


class Wide:
    def __init__(self, planes, places, pos, ya_ref, yb_ref, za_ref, zb_ref):
        self.planes, self.places = planes, places
        self.rows = Rows(pos, places, ya_ref, yb_ref)
        z = Pair(pos, 2, za_ref, zb_ref)
        groups = za_ref.shape[0]
        self.behind = [z.below(g) for g in range(groups)]
        self.ahead = [z.above(g) for g in range(groups)]

    def __call__(self, k):
        lane = iota((PY, CZ), 1)
        side = jnp.zeros((PY, CZ), F32)
        if k in self.places:
            at, off, width = self.places[k]
            group, start = at // 16, at % 16 * 8 + off
            ahead = turn(self.ahead[group], -start, 1)
            behind = turn(self.behind[group], -start - width, 1)
            side = jnp.where(lane < 8, ahead, jnp.where(lane >= CZ - 8, behind, 0.0))
        middle = jnp.concatenate([self.rows.below(k), self.planes[k](pl.ds(0, CY)), self.rows.above(k)], axis=0)
        return jnp.concatenate([middle, side], axis=1)


def first_amounts_kernel(sums_ref, matrix_ref, out_ref):
    out_ref[...] = coarse_rows(matrix_ref, sums_ref[pl.ds(0, 64, stride=2), :], sums_ref[pl.ds(1, 64, stride=2), :])


def store(ref, i, j, value, halo):
    if max(HX - i, i - HX - CX + 1) >= halo:
        ref[i, j, :, 0:CZ] = value[:, 0:CZ]
    else:
        ref[i, j] = value


def chebyshev(halo, w_ref, rp_ref, a_ref, b_ref):
    _, weights = recurrence()
    now, before = a_ref, b_ref
    for index, (keep, push) in enumerate(weights):
        halo -= 1
        for i in range(HX - halo, HX + CX + halo):
            for j in range(ROWS):
                around = around_strided(lambda i, j: now[i, j], i, j)
                total = rp_ref[i, j]
                for d in range(6):
                    total = total + w_ref[d, i, j] * around[d]
                new = (1.0 + keep - push) * now[i, j] + push * total
                if index:
                    new = new - keep * before[i, j]
                store(before, i, j, new, halo)
        now, before = before, now
    return now


def smooth_kernel(
    pos, r_ref, g_in, v_in, xa_ref, xb_ref, ya_ref, yb_ref, za_ref, zb_ref, amounts_ref,
    p_ref, xa_out, xb_out, vx_ref, w_ref, diag_ref,
    g_ref, wide_ref, rp_ref, a_ref, b_ref, nat_ref,
):
    planes = stacked_planes(r_ref, g_in, v_in, Pair(pos, 0, xa_ref, xb_ref))
    wide = Wide(planes, PLACES_1[0], pos, ya_ref, yb_ref, za_ref, zb_ref)
    mask = inside_yz(pos)
    for i in range(PX):
        put(g_ref, i, jnp.where(wide(N_R + i) > 0.5, mask * inside_x(pos, i - HX), 0.0))
    for i in range(N_V):
        put(vx_ref, i, wide(N_R + N_G + i) * (mask * inside_x(pos, i - H_V)))
    for k in range(N_R):
        put(wide_ref, k, wide(k))
    first_scale, _ = recurrence()
    for j in range(ROWS):
        mask = inside_yz(pos, j)
        for i in range(1, PX - 1):
            labels = around_strided(lambda i, j: strided(g_ref, i, j), i, j)
            first, second = pair(strided(g_ref, i, j))
            count = (labels[0] + labels[1]) + (labels[2] + labels[3]) + (labels[4] + labels[5])
            diagonal = 6.0 * first + second * count
            if HX <= i < HX + CX:
                diag_ref[i - HX, j] = diagonal[:, 0:CZ]
            inverse = mask * inside_x(pos, i - HX) / diagonal
            first, second = first * inverse, second * inverse
            for d in range(6):
                w_ref[d, i, j] = first + second * labels[d]
            if HX - H_R <= i < HX + CX + H_R:
                scaled = strided(wide_ref, i - HX + H_R, j) * inverse
                store(rp_ref, i, j, scaled, H_R)
                store(a_ref, i, j, scaled * first_scale, H_R)
    result = chebyshev(H_R, w_ref, rp_ref, a_ref, b_ref)
    for j in range(ROWS):
        for x in range(CX):
            nat_ref[x, pl.ds(j, 8, stride=ROWS), :] = result[HX + x, j, :, 0:CZ]
    (field,) = fields([amounts_ref[...]])
    for x in range(CX):
        p_ref[x] = nat_ref[x, HY : HY + CY] + v_in[x] * plane_field(field, x // 2)
    even = is_even(pos, 0)
    for k in range(HX):
        put_pair(even, xa_out, xb_out, k, p_ref[k], p_ref[CX - HX + k])


def product_kernel(vx_ref, w_ref, diag_ref, out_ref, acc_ref):
    for j in range(ROWS):
        rows = pl.ds(j, 8, stride=ROWS)
        last_y = (iota((8, CZ), 0) * ROWS + j - HY) % 16 == 15
        last_z = iota((8, CZ), 1) % 32 == 31
        for sx in range(4):
            sums = [jnp.zeros((8, CZ), F32) for _ in range(4)]
            for x in (2 * sx, 2 * sx + 1):
                mine = strided(vx_ref, x + H_V, j)
                ahead = (
                    strided(vx_ref, x + H_V + 1, j),
                    strided(vx_ref, x + H_V, j + 1) if j < ROWS - 1 else pltpu.roll(strided(vx_ref, x + H_V, 0), 7, 0),
                    pltpu.roll(mine, PZ - 1, 1),
                )
                scaled = diag_ref[x, j] * mine[:, 0:CZ]
                cross = [scaled * w_ref[2 * d + 1, x + HX, j, :, 0:CZ] * ahead[d][:, 0:CZ] for d in range(3)]
                inner = jnp.where(last_y, 0.0, cross[1]) + jnp.where(last_z, 0.0, cross[2])
                if x % 2 == 0:
                    inner = inner + cross[0]
                else:
                    sums[1] = sums[1] - cross[0]
                sums[0] = sums[0] + (scaled * mine[:, 0:CZ] - 2.0 * inner)
                sums[2] = sums[2] - jnp.where(last_y, cross[1], 0.0)
                sums[3] = sums[3] - jnp.where(last_z, cross[2], 0.0)
            for n in range(4):
                acc_ref[4 * n + sx, rows, :] = sums[n]
    quads = row_sums([[acc_ref[4 * n + sx, HY : HY + CY] for sx in range(4)] for n in range(4)])
    for n in range(4):
        out_ref[n : n + 1] = quads[n]


def image_of(ref, w_ref, diag_ref, x, j):
    values = around_strided(lambda i, j: ref[i, j], x + HX, j)
    mine = ref[x + HX, j]
    total = w_ref[0, x + HX, j] * (mine - values[0])
    for d in range(1, 6):
        total = total + w_ref[d, x + HX, j] * (mine - values[d])
    return mine[:, 0:CZ], total[:, 0:CZ] * diag_ref[x, j]


def twice(x, half):
    lane = iota(x.shape, 1)
    other = pltpu.roll(x, ND, 1)
    return jnp.where(lane < ND, x, other) if half == 0 else jnp.where(lane < ND, other, x)


def ahead_behind(x, step, sign):
    lane = iota(x.shape, 1)
    stride, devices = ((16, 32), (4, 8), (1, 1))[step]
    place = (lane // stride) % 4
    near = pltpu.roll(x, (128 - stride * sign) % 128, 1)
    far = pltpu.roll(x, (3 * stride * sign) % 128, 1)
    far = pltpu.roll(far, (NDEV - devices * sign) % NDEV, 0)
    return jnp.where(place != (3 if sign > 0 else 0), near, far)


def image_kernel(
    pos, p_ref, xa_ref, xb_ref, ya_ref, yb_ref, za_ref, zb_ref, w_ref, diag_ref, r_ref, v_ref, e_ref,
    q_ref, c_ref, y_ref, send_ref,
    full_ref, plane_ref, rp_ref, a_ref, b_ref,
):
    planes = padded_planes(p_ref, Pair(pos, 0, xa_ref, xb_ref))
    wide = Wide(planes, PLACES_2[0], pos, ya_ref, yb_ref, za_ref, zb_ref)
    mask = inside_yz(pos)
    for i in range(PX):
        put(full_ref, i, wide(i) * (mask * inside_x(pos, i - HX)))
    first_scale, _ = recurrence()
    for j in range(ROWS):
        rows = pl.ds(j, 8, stride=ROWS)
        for i in range(1, PX - 1):
            values = around_strided(lambda i, j: strided(full_ref, i, j), i, j)
            mine = strided(full_ref, i, j)
            total = w_ref[0, i, j] * (mine - values[0])
            for d in range(1, 6):
                total = total + w_ref[d, i, j] * (mine - values[d])
            store(rp_ref, i, j, total, HX - 1)
            store(a_ref, i, j, total * first_scale, HX - 1)
            if HX <= i < HX + CX:
                plane_ref[i - HX, rows, :] = total[:, 0:CZ] * diag_ref[i - HX, j]
    result = chebyshev(HX - 1, w_ref, rp_ref, a_ref, b_ref)
    for x in range(CX):
        for j in range(ROWS):
            rows = pl.ds(j, 8, stride=ROWS)
            mine, image = image_of(result, w_ref, diag_ref, x, j)
            plane_ref[CX + x, rows, :] = mine
            plane_ref[2 * CX + x, rows, :] = image
    parts = [jnp.zeros((CY, CZ), F32) for _ in range(4)]
    energy = jnp.zeros((CY, CZ), F32)
    curve = jnp.zeros((CY, CZ), F32)
    for x in range(CX):
        q, c, y = (plane_ref[CX * n + x, HY : HY + CY] for n in range(3))
        q_ref[x], c_ref[x], y_ref[x] = q, c, y
        energy = energy + r_ref[x] * p_ref[x]
        curve = curve + q * p_ref[x]
        parts[x // 2] = parts[x // 2] + v_ref[x] * q
    lane = iota((1, 128), 1)
    scalars = jnp.where(lane == 64, total_sum(energy), jnp.where(lane == 65, total_sum(curve), 0.0))
    (row,) = row_sums([parts])
    send = jnp.concatenate(
        [
            jnp.where(lane < ND, row, e_ref[0:1]),
            jnp.where(lane < ND, e_ref[1:2], e_ref[2:3]),
            jnp.where(lane < ND, e_ref[3:4], scalars),
        ],
        axis=1,
    )
    send_ref[...] = jnp.broadcast_to(send, (NDEV, 384))


def first_scalars(sums_ref):
    totals = jnp.sum(sums_ref[:, 256:384], axis=0, keepdims=True)
    energy = totals[0:1, 64:65]
    curve = totals[0:1, 65:66]
    return energy, curve, energy / curve


def amounts_kernel(sums_ref, matrix_ref, p_ref, q_ref, c_ref, y_ref, v_ref, r_ref, send_ref, piece_ref):
    _, _, alpha = first_scalars(sums_ref)
    piece_ref[...] = sums_ref[:, 0:128]
    even = piece_ref[pl.ds(0, 64, stride=2), :]
    odd = pltpu.roll(piece_ref[pl.ds(1, 64, stride=2), :], 64, 1)
    amounts = coarse_rows(matrix_ref, even, odd)
    (field,) = fields([amounts])
    sums = [jnp.zeros((CY, CZ), F32) for _ in range(3)]
    for x in range(CX):
        lifted = v_ref[x] * plane_field(field, x // 2)
        p, q, c = p_ref[x], q_ref[x], c_ref[x]
        residual = r_ref[x] - alpha * q
        smooth = p - alpha * c
        smooth_image = q - alpha * y_ref[x]
        precond = smooth - alpha * lifted
        sums[0] = sums[0] + residual * precond
        sums[1] = sums[1] + precond * q
        sums[2] = sums[2] + smooth_image * (smooth - 2.0 * alpha * lifted)
    lane = iota((1, 128), 1)
    row = jnp.where(lane < ND, amounts, 0.0)
    for n in range(3):
        row = jnp.where(lane == ND + n, total_sum(sums[n]), row)
    send_ref[...] = jnp.broadcast_to(row, (NDEV, 128))


def final_kernel(
    pos, sums_ref, got_ref, p_ref, q_ref, c_ref, y_ref, r_ref, vx_ref, w_ref, diag_ref,
    pressure_ref, residual_ref,
    lift_ref, plane_ref,
):
    energy, curve, alpha = first_scalars(sums_ref)
    got = got_ref[...]
    dup = twice(got, 0)
    half = twice(sums_ref[:, 0:128], 1) * dup
    towards = (twice(sums_ref[:, 128:256], 0), twice(sums_ref[:, 128:256], 1), twice(sums_ref[:, 256:384], 0))
    for step in range(3):
        half = half + 2.0 * towards[step] * ahead_behind(dup, step, 1)
    quad = total_sum(jnp.where(iota((NDEV, 128), 1) < ND, half * dup, 0.0))
    totals = jnp.sum(got, axis=0, keepdims=True)
    energy_next = totals[0:1, 64:65]
    mixed = totals[0:1, 65:66]
    beta = energy_next / energy
    curve_next = totals[0:1, 66:67] + alpha * alpha * quad + 2.0 * beta * mixed + beta * beta * curve
    alpha_next = energy_next / curve_next

    me = (pos[0] * 4 + pos[1]) * 8 + pos[2]
    rows = []
    for shift in (0, -32, 32, -8, 8, -1, 1):
        at = jnp.clip(me + shift, 0, NDEV - 1)
        rows.append(got_ref[pl.ds(at, 1), :])
    mine, xm, xp, ym, yp, zm, zp = fields(rows)
    lanes = iota((PY, CZ), 1)
    zeros = jnp.zeros((HY, CZ), F32)
    for i in range(N_V):
        x = i - H_V
        if x < 0 or x >= CX:
            own = plane_field(xm, 3) if x < 0 else plane_field(xp, 0)
            middle = jnp.concatenate([zeros, own, zeros], axis=0)
            side = jnp.zeros((PY, CZ), F32)
        else:
            s = x // 2
            down = jnp.broadcast_to(ym[4 * s + 3 : 4 * s + 4], (HY, CZ))
            up = jnp.broadcast_to(yp[4 * s : 4 * s + 1], (HY, CZ))
            middle = jnp.concatenate([down, plane_field(mine, s), up], axis=0)
            ahead = jnp.concatenate([zeros, plane_field(zp, s), zeros], axis=0)
            behind = jnp.concatenate([zeros, plane_field(zm, s), zeros], axis=0)
            side = jnp.where(lanes < 8, ahead, jnp.where(lanes >= CZ - 8, behind, 0.0))
        lift_ref[0, i] = vx_ref[0, i] * middle
        lift_ref[1, i] = vx_ref[1, i] * side
    for x in range(CX):
        for j in range(ROWS):
            values = around_strided(lambda i, j: strided(lift_ref, i, j), x + H_V, j)
            mine = strided(lift_ref, x + H_V, j)
            total = w_ref[0, x + HX, j] * (mine - values[0])
            for d in range(1, 6):
                total = total + w_ref[d, x + HX, j] * (mine - values[d])
            plane_ref[x, pl.ds(j, 8, stride=ROWS), :] = total[:, 0:CZ] * diag_ref[x, j]
        lifted_image = plane_ref[x, HY : HY + CY]
        lifted = lift_ref[0, x + H_V, HY : HY + CY]
        p, q = p_ref[x], q_ref[x]
        precond = p - alpha * (c_ref[x] + lifted)
        precond_image = q - alpha * (y_ref[x] + lifted_image)
        direction = precond + beta * p
        image = precond_image + beta * q
        pressure_ref[x] = alpha * p + alpha_next * direction
        residual_ref[x] = (r_ref[x] - alpha * q) - alpha_next * image


VMEM = pl.BlockSpec(memory_space=pltpu.VMEM)
SMEM = pl.BlockSpec(memory_space=pltpu.SMEM)


def call(kernel, outs, scratch=(), smem=False, hbm=0, mib=20, cost=None):
    def run(*args):
        many = isinstance(outs, list)
        specs = [VMEM] * len(args)
        if smem:
            specs[0] = SMEM
        for n in range(int(smem), int(smem) + hbm):
            specs[n] = pl.BlockSpec(memory_space=pltpu.HBM)
        return pl.pallas_call(
            kernel,
            out_shape=[jax.ShapeDtypeStruct(s, F32) for s in outs] if many else jax.ShapeDtypeStruct(outs, F32),
            in_specs=specs,
            out_specs=[VMEM] * len(outs) if many else VMEM,
            scratch_shapes=[pltpu.VMEM(s, F32) if isinstance(s, tuple) else s for s in scratch],
            compiler_params=pltpu.CompilerParams(vmem_limit_bytes=mib * 1024 * 1024),
            cost_estimate=cost,
        )(*args)

    return run


def cost(us):
    return pl.CostEstimate(flops=int(us * 1e6), bytes_accessed=int(us * 3e6), transcendentals=0)


def swap(a, b, axis):
    count = lax.axis_size(axis)
    got_a = lax.ppermute(a, axis, [(i, i ^ 1) for i in range(count)])
    got_b = lax.ppermute(b, axis, [(i, (i - 1 if i % 2 == 0 else i + 1) % count) for i in range(count)])
    return got_a, got_b


def gather(rows):
    return lax.all_to_all(rows, AXES, 0, 0, tiled=True)


def exchange_yz(pos, own):
    places, count = PLACES_2 if len(own) == 3 else PLACES_1
    groups = -(-count // 16)
    ya, yb = call(y_kernel, [(count, HY, CZ)] * 2, smem=True)(pos, *own)
    ya, yb = swap(ya, yb, "gy")
    left, right = call(z_own_kernel, [(groups, CY, CZ)] * 2, smem=True, cost=cost(1))(pos, *own)
    pack = functools.partial(z_kernel, places)
    za, zb = call(pack, [(groups, PY, CZ)] * 2, smem=True)(pos, ya, yb, left, right)
    return (ya, yb, *swap(za, zb, "gz"))


def local(right_side, phase, deflation_weights, coarse_inverse):
    pos = jnp.stack([lax.axis_index(a) for a in AXES]).astype(jnp.int32)
    block = (CX, CY, CZ)
    tall = (2, PX, PY, CZ)
    split = (PX, ROWS, 8, PZ)
    n_x = H_R + H_G + H_V
    labels = jnp.where(phase == 1, 1.0, 0.0).astype(F32)
    xa, xb, send, r, g, v = call(
        start_kernel,
        [(n_x, CY, CZ), (n_x, CY, CZ), (NDEV, 128), block, block, block],
        smem=True,
    )(pos, jnp.concatenate([right_side, labels, deflation_weights], axis=0))
    xa, xb = swap(xa, xb, "gx")
    sums = gather(send)
    xa, xb, sums = lax.optimization_barrier((xa, xb, sums))
    own = (r, g, v, xa, xb)
    halos = exchange_yz(pos, own)
    amounts = call(first_amounts_kernel, (1, 128), cost=cost(1))(sums, coarse_inverse)
    p, xa, xb, v_wide, w, diag = call(
        smooth_kernel,
        [block, (HX, CY, CZ), (HX, CY, CZ), (2, N_V, PY, CZ), (6, *split), (CX, ROWS, 8, CZ)],
        scratch=[tall, (2, N_R, PY, CZ), split, split, split, (CX, PY, CZ)],
        smem=True,
    )(pos, *own, *halos, amounts)
    own = (p, *swap(xa, xb, "gx"))
    quads = call(product_kernel, (4, 128), scratch=[(16, PY, CZ)], cost=cost(1))(v_wide, w, diag)
    halos = exchange_yz(pos, own)
    q, c, y, send = call(
        image_kernel,
        [block, block, block, (NDEV, 384)],
        scratch=[tall, (3 * CX, PY, CZ), split, split, split],
        smem=True,
    )(pos, *own, *halos, w, diag, r, v, quads)
    sums = gather(send)
    send = call(amounts_kernel, (NDEV, 128), scratch=[(NDEV, 128)])(sums, coarse_inverse, p, q, c, y, v, r)
    got = gather(send)
    pressure, residual = call(
        final_kernel, [block, block], scratch=[(2, N_V, PY, CZ), (CX, PY, CZ)], smem=True
    )(pos, sums, got, p, q, c, y, r, v_wide, w, diag)
    return (pressure, residual)


def solution(mesh):
    return jax.shard_map(
        local,
        mesh=mesh,
        in_specs=(P(*AXES), P(*AXES), P(*AXES), P(AXES, None)),
        out_specs=(P(*AXES), P(*AXES)),
        check_vma=False,
    )
```

```python
import functools

import jax
import jax.numpy as jnp
import numpy as np
from jax import lax
from jax.experimental import pallas as pl
from jax.experimental.pallas import tpu as pltpu
from jax.sharding import PartitionSpec as P

AXES = ("gx", "gy", "gz")
SBX = 4
ND = 64
DEG = 6
spectrum_low = 0.08
spectrum_high = 2.0

CX, CY, CZ = 8, 64, 128
HX, HY = 7, 8
PX, PY, PZ = CX + 2 * HX, CY + 2 * HY, 2 * CZ
H_R, H_G, H_V = 5, 7, 1
N_R, N_G, N_V = CX + 2 * H_R, CX + 2 * H_G, CX + 2 * H_V
N_ALL = N_R + N_G + N_V
NDEV = 128
ROWS = PY // 8

LIQUID = np.float32(1.0)
GAS = np.float32(0.001)
F_LL = np.float32(2.0) / (LIQUID + LIQUID)
F_LG = np.float32(2.0) / (LIQUID + GAS)
F_GG = np.float32(2.0) / (GAS + GAS)

def strips(widths):
    room, places = [], {}
    for k, width in sorted(enumerate(widths), key=lambda item: -item[1]):
        if width <= 0:
            continue
        at = next((n for n, free in enumerate(room) if free >= width), len(room))
        if at == len(room):
            room.append(8)
        places[k] = (at, 8 - room[at], width)
        room[at] -= width
    return places, len(room)


def reach(halo, extent):
    return [extent - max(0, -rel, rel - CX + 1) for rel in range(-halo, CX + halo)]


PLACES_1 = strips(reach(H_R, H_R) + reach(H_G, H_G) + reach(H_V, H_V))
PLACES_2 = strips(reach(HX, HX))

F32 = jnp.float32
EXACT = lax.Precision.HIGHEST


def recurrence():
    center = 0.5 * (spectrum_high + spectrum_low)
    half_width = 0.5 * (spectrum_high - spectrum_low)
    ratio = center / half_width
    earlier = 1.0 / ratio
    weights = []
    for index in range(DEG - 1):
        later = 1.0 / (2.0 * ratio - earlier)
        weights.append((later * earlier, 2.0 * later / half_width))
        earlier = later
    return (1.0 / center, weights)


def iota(shape, dim):
    return lax.broadcasted_iota(jnp.int32, shape, dim)


def whole(ref, i):
    return jnp.concatenate([ref[0, i], ref[1, i]], axis=1)


def put(ref, i, plane):
    ref[0, i] = plane[:, 0:CZ]
    ref[1, i] = plane[:, CZ:PZ]


def neighbours(ref, i):
    v = whole(ref, i)
    return (
        whole(ref, i - 1),
        whole(ref, i + 1),
        pltpu.roll(v, 1, 0),
        pltpu.roll(v, PY - 1, 0),
        pltpu.roll(v, 1, 1),
        pltpu.roll(v, PZ - 1, 1),
    )


def strided(ref, i, j):
    rows = pl.ds(j, 8, stride=ROWS)
    return jnp.concatenate([ref[0, i, rows, :], ref[1, i, rows, :]], axis=1)


def around_strided(load, i, j):
    v = load(i, j)
    return (
        load(i - 1, j),
        load(i + 1, j),
        load(i, j - 1) if j else pltpu.roll(load(i, ROWS - 1), 1, 0),
        load(i, j + 1) if j < ROWS - 1 else pltpu.roll(load(i, 0), 7, 0),
        pltpu.roll(v, 1, 1),
        pltpu.roll(v, PZ - 1, 1),
    )


def inside_yz(pos, j=None):
    gy, gz = pos[1], pos[2]
    shape = (PY, PZ) if j is None else (8, PZ)
    row = iota(shape, 0) if j is None else iota(shape, 0) * ROWS + j
    row = row - HY + gy * CY
    lane = iota(shape, 1)
    near = jnp.where(lane < CZ + CZ // 2, lane, lane - PZ) + gz * CZ
    kept = (lane < CZ + 8) | (lane >= PZ - 8)
    good = (row >= 0) & (row < 4 * CY) & (near >= 0) & (near < 8 * CZ) & kept
    return jnp.where(good, 1.0, 0.0).astype(F32)


def inside_x(pos, rel):
    x = pos[0] * CX + rel
    return jnp.where((x >= 0) & (x < 4 * CX), 1.0, 0.0).astype(F32)


def pair(labels):
    gas = labels > 0.5
    return jnp.where(gas, F_LG, F_LL), jnp.where(gas, F_GG - F_LG, F_LG - F_LL)


def row_sums(arrays):
    rows = []
    for parts in arrays:
        for part in parts:
            for sy in range(4):
                rows.append(jnp.sum(part[16 * sy : 16 * sy + 16], axis=0, keepdims=True))
    stacked = jnp.concatenate(rows, axis=0)
    pick = jnp.where(iota((128, 128), 0) // 32 == iota((128, 128), 1) % 4, 1.0, 0.0).astype(F32)
    spread = jnp.dot(stacked, pick, precision=EXACT, preferred_element_type=F32)
    keep = (iota((16, 128), 1) // 4) % 16 == iota((16, 128), 0)
    return [
        jnp.sum(jnp.where(keep, spread[16 * n : 16 * n + 16], 0.0), axis=0, keepdims=True) for n in range(len(arrays))
    ]


def fields(rows):
    count = len(rows)
    keep = (iota((16, 128), 1) // 4 == iota((16, 128), 0)) & (iota((16, 128), 1) < ND)
    tall = jnp.concatenate([jnp.where(keep, jnp.broadcast_to(r, (16, 128)), 0.0) for r in rows], axis=0)
    pick = jnp.where(iota((128, 128), 0) % 4 == iota((128, 128), 1) // 32, 1.0, 0.0).astype(F32)
    out = jnp.dot(tall, pick, precision=EXACT, preferred_element_type=F32)
    return [out[16 * k : 16 * k + 16] for k in range(count)]


def plane_field(field, sx):
    return jnp.concatenate(
        [jnp.broadcast_to(field[4 * sx + sy : 4 * sx + sy + 1], (16, 128)) for sy in range(4)], axis=0
    )


def coarse_rows(matrix_ref, even, odd):
    wide = jnp.where(iota((64, 128), 1) < ND, even, odd)
    total = matrix_ref[:, 0:128] * wide[0:1]
    for t in range(1, 64):
        total = total + matrix_ref[:, 128 * t : 128 * t + 128] * wide[t : t + 1]
    column = jnp.sum(total, axis=1, keepdims=True)
    keep = iota((64, 128), 1) % ND == iota((64, 128), 0)
    return jnp.sum(jnp.where(keep, column, 0.0), axis=0, keepdims=True)


def total_sum(x):
    return jnp.sum(jnp.sum(x, axis=0, keepdims=True), axis=1, keepdims=True)


def start_kernel(pos, all_ref, xa_ref, xb_ref, send_ref, r_ref, g_ref, v_ref):
    r_ref[...] = all_ref[0:CX]
    g_ref[...] = all_ref[CX : 2 * CX]
    v_ref[...] = all_ref[2 * CX :]
    parts = []
    for sx in range(4):
        parts.append(r_ref[2 * sx] * v_ref[2 * sx] + r_ref[2 * sx + 1] * v_ref[2 * sx + 1])
    (row,) = row_sums([parts])
    send_ref[...] = jnp.broadcast_to(row, (NDEV, 128))
    even = is_even(pos, 0)
    for base, ref, halo in ((0, r_ref, H_R), (H_R, g_ref, H_G), (H_R + H_G, v_ref, H_V)):
        for k in range(halo):
            put_pair(even, xa_ref, xb_ref, base + k, ref[k], ref[CX - halo + k])


def is_even(pos, axis):
    return (pos[axis] & 1) == 0


def put_pair(even, a_ref, b_ref, k, down, up):
    a_ref[k] = jnp.where(even, up, down)
    b_ref[k] = jnp.where(even, down, up)


class Pair:
    def __init__(self, pos, axis, a_ref, b_ref):
        self.even, self.a, self.b = is_even(pos, axis), a_ref, b_ref

    def below(self, *at):
        return jnp.where(self.even, self.b[at], self.a[at])

    def above(self, *at):
        return jnp.where(self.even, self.a[at], self.b[at])


def stacked_planes(r_ref, g_ref, v_ref, sides):
    planes = []
    for halo, ref, base in ((H_R, r_ref, 0), (H_G, g_ref, H_R), (H_V, v_ref, H_R + H_G)):
        for rel in range(-halo, CX + halo):
            if rel < 0:
                planes.append(lambda s, k=base + rel + halo: sides.below(k, s))
            elif rel >= CX:
                planes.append(lambda s, k=base + rel - CX: sides.above(k, s))
            else:
                planes.append(lambda s, k=rel, ref=ref: ref[k, s])
    return planes


def padded_planes(p_ref, sides):
    planes = []
    for rel in range(-HX, CX + HX):
        if rel < 0:
            planes.append(lambda s, k=rel + HX: sides.below(k, s))
        elif rel >= CX:
            planes.append(lambda s, k=rel - CX: sides.above(k, s))
        else:
            planes.append(lambda s, k=rel: p_ref[k, s])
    return planes


def all_planes(refs, pos):
    sides = Pair(pos, 0, *refs[-2:])
    return padded_planes(refs[0], sides) if len(refs) == 3 else stacked_planes(*refs[:3], sides)


def places_of(refs):
    return PLACES_2[0] if len(refs) == 3 else PLACES_1[0]


def turn(x, shift, axis):
    shift %= x.shape[axis]
    return pltpu.roll(x, shift, axis) if shift else x


def y_kernel(pos, *refs):
    refs, (a_ref, b_ref) = refs[:-2], refs[-2:]
    even = is_even(pos, 1)
    planes = all_planes(refs, pos)
    row = iota((HY, CZ), 0)
    tiles = {}
    for k, (at, off, width) in places_of(refs).items():
        down, up = tiles.get(at, (jnp.zeros((HY, CZ), F32),) * 2)
        here = (row >= off) & (row < off + width)
        down = jnp.where(here, turn(planes[k](pl.ds(0, HY)), off, 0), down)
        up = jnp.where(here, turn(planes[k](pl.ds(CY - HY, HY)), off + width, 0), up)
        tiles[at] = (down, up)
    for at, (down, up) in tiles.items():
        put_pair(even, a_ref, b_ref, at, down, up)


def pack_lanes(value, places, rows):
    lane = iota((rows, CZ), 1)
    packed = {}
    for k, (at, off, width) in places.items():
        group, start = at // 16, at % 16 * 8 + off
        left, right = packed.get(group, (jnp.zeros((rows, CZ), F32),) * 2)
        here = (lane >= start) & (lane < start + width)
        left = jnp.where(here, turn(value(k), start, 1), left)
        right = jnp.where(here, turn(value(k), start + width, 1), right)
        packed[group] = (left, right)
    return packed


def z_own_kernel(pos, *refs):
    refs, (left_ref, right_ref) = refs[:-2], refs[-2:]
    planes = all_planes(refs, pos)
    for group, (left, right) in pack_lanes(lambda k: planes[k](pl.ds(0, CY)), places_of(refs), CY).items():
        left_ref[group] = left
        right_ref[group] = right


class Rows:
    def __init__(self, pos, places, a_ref, b_ref):
        self.pair, self.places = Pair(pos, 1, a_ref, b_ref), places

    def below(self, k):
        if k not in self.places:
            return jnp.zeros((HY, CZ), F32)
        at, off, width = self.places[k]
        return turn(self.pair.below(at), -off - width, 0)

    def above(self, k):
        if k not in self.places:
            return jnp.zeros((HY, CZ), F32)
        at, off, _ = self.places[k]
        return turn(self.pair.above(at), -off, 0)


def z_kernel(places, pos, ya_ref, yb_ref, left_ref, right_ref, za_ref, zb_ref):
    even = is_even(pos, 2)
    rows = Rows(pos, places, ya_ref, yb_ref)
    below = pack_lanes(rows.below, places, HY)
    above = pack_lanes(rows.above, places, HY)
    for group in below:
        left = jnp.concatenate([below[group][0], left_ref[group], above[group][0]], axis=0)
        right = jnp.concatenate([below[group][1], right_ref[group], above[group][1]], axis=0)
        put_pair(even, za_ref, zb_ref, group, left, right)


class Wide:
    def __init__(self, planes, places, pos, ya_ref, yb_ref, za_ref, zb_ref):
        self.planes, self.places = planes, places
        self.rows = Rows(pos, places, ya_ref, yb_ref)
        z = Pair(pos, 2, za_ref, zb_ref)
        groups = za_ref.shape[0]
        self.behind = [z.below(g) for g in range(groups)]
        self.ahead = [z.above(g) for g in range(groups)]

    def __call__(self, k):
        lane = iota((PY, CZ), 1)
        side = jnp.zeros((PY, CZ), F32)
        if k in self.places:
            at, off, width = self.places[k]
            group, start = at // 16, at % 16 * 8 + off
            ahead = turn(self.ahead[group], -start, 1)
            behind = turn(self.behind[group], -start - width, 1)
            side = jnp.where(lane < 8, ahead, jnp.where(lane >= CZ - 8, behind, 0.0))
        middle = jnp.concatenate([self.rows.below(k), self.planes[k](pl.ds(0, CY)), self.rows.above(k)], axis=0)
        return jnp.concatenate([middle, side], axis=1)


def first_amounts_kernel(sums_ref, matrix_ref, out_ref):
    out_ref[...] = coarse_rows(matrix_ref, sums_ref[pl.ds(0, 64, stride=2), :], sums_ref[pl.ds(1, 64, stride=2), :])


def store(ref, i, j, value, halo):
    if max(HX - i, i - HX - CX + 1) >= halo:
        ref[i, j, :, 0:CZ] = value[:, 0:CZ]
    else:
        ref[i, j] = value


def chebyshev(halo, w_ref, rp_ref, a_ref, b_ref, steps=(0, DEG - 1), into=None):
    _, weights = recurrence()
    now, before = a_ref, b_ref
    for index in range(*steps):
        keep, push = weights[index]
        halo -= 1
        out = into.pop(0) if into else before
        for i in range(HX - halo, HX + CX + halo):
            for j in range(ROWS):
                around = around_strided(lambda i, j: now[i, j], i, j)
                total = rp_ref[i, j]
                for d in range(6):
                    total = total + w_ref[d, i, j] * around[d]
                new = (1.0 + keep - push) * now[i, j] + push * total
                if index:
                    new = new - keep * before[i, j]
                store(out, i, j, new, halo)
        now, before = out, now
    return now, before


def smooth_kernel(
    pos, r_ref, g_in, v_in, xa_ref, xb_ref, ya_ref, yb_ref, za_ref, zb_ref, amounts_ref,
    p_ref, xa_out, xb_out, vx_ref, w_ref, diag_ref,
    g_ref, wide_ref, rp_ref, a_ref, b_ref, nat_ref,
):
    planes = stacked_planes(r_ref, g_in, v_in, Pair(pos, 0, xa_ref, xb_ref))
    wide = Wide(planes, PLACES_1[0], pos, ya_ref, yb_ref, za_ref, zb_ref)
    mask = inside_yz(pos)
    for i in range(PX):
        put(g_ref, i, jnp.where(wide(N_R + i) > 0.5, mask * inside_x(pos, i - HX), 0.0))
    for i in range(N_V):
        put(vx_ref, i, wide(N_R + N_G + i) * (mask * inside_x(pos, i - H_V)))
    for k in range(N_R):
        put(wide_ref, k, wide(k))
    first_scale, _ = recurrence()
    for j in range(ROWS):
        mask = inside_yz(pos, j)
        for i in range(1, PX - 1):
            labels = around_strided(lambda i, j: strided(g_ref, i, j), i, j)
            first, second = pair(strided(g_ref, i, j))
            count = (labels[0] + labels[1]) + (labels[2] + labels[3]) + (labels[4] + labels[5])
            diagonal = 6.0 * first + second * count
            if HX <= i < HX + CX:
                diag_ref[i - HX, j] = diagonal[:, 0:CZ]
            inverse = mask * inside_x(pos, i - HX) / diagonal
            first, second = first * inverse, second * inverse
            for d in range(6):
                w_ref[d, i, j] = first + second * labels[d]
            if HX - H_R <= i < HX + CX + H_R:
                scaled = strided(wide_ref, i - HX + H_R, j) * inverse
                store(rp_ref, i, j, scaled, H_R)
                store(a_ref, i, j, scaled * first_scale, H_R)
    result, _ = chebyshev(H_R, w_ref, rp_ref, a_ref, b_ref)
    for j in range(ROWS):
        for x in range(CX):
            nat_ref[x, pl.ds(j, 8, stride=ROWS), :] = result[HX + x, j, :, 0:CZ]
    (field,) = fields([amounts_ref[...]])
    for x in range(CX):
        p_ref[x] = nat_ref[x, HY : HY + CY] + v_in[x] * plane_field(field, x // 2)
    even = is_even(pos, 0)
    for k in range(HX):
        put_pair(even, xa_out, xb_out, k, p_ref[k], p_ref[CX - HX + k])


def product_kernel(vx_ref, w_ref, diag_ref, out_ref, acc_ref):
    for j in range(ROWS):
        rows = pl.ds(j, 8, stride=ROWS)
        last_y = (iota((8, CZ), 0) * ROWS + j - HY) % 16 == 15
        last_z = iota((8, CZ), 1) % 32 == 31
        for sx in range(4):
            sums = [jnp.zeros((8, CZ), F32) for _ in range(4)]
            for x in (2 * sx, 2 * sx + 1):
                mine = strided(vx_ref, x + H_V, j)
                ahead = (
                    strided(vx_ref, x + H_V + 1, j),
                    strided(vx_ref, x + H_V, j + 1) if j < ROWS - 1 else pltpu.roll(strided(vx_ref, x + H_V, 0), 7, 0),
                    pltpu.roll(mine, PZ - 1, 1),
                )
                scaled = diag_ref[x, j] * mine[:, 0:CZ]
                cross = [scaled * w_ref[2 * d + 1, x + HX, j, :, 0:CZ] * ahead[d][:, 0:CZ] for d in range(3)]
                inner = jnp.where(last_y, 0.0, cross[1]) + jnp.where(last_z, 0.0, cross[2])
                if x % 2 == 0:
                    inner = inner + cross[0]
                else:
                    sums[1] = sums[1] - cross[0]
                sums[0] = sums[0] + (scaled * mine[:, 0:CZ] - 2.0 * inner)
                sums[2] = sums[2] - jnp.where(last_y, cross[1], 0.0)
                sums[3] = sums[3] - jnp.where(last_z, cross[2], 0.0)
            for n in range(4):
                acc_ref[4 * n + sx, rows, :] = sums[n]
    quads = row_sums([[acc_ref[4 * n + sx, HY : HY + CY] for sx in range(4)] for n in range(4)])
    for n in range(4):
        out_ref[n : n + 1] = quads[n]


def image_of(ref, w_ref, diag_ref, x, j):
    values = around_strided(lambda i, j: ref[i, j], x + HX, j)
    mine = ref[x + HX, j]
    total = w_ref[0, x + HX, j] * (mine - values[0])
    for d in range(1, 6):
        total = total + w_ref[d, x + HX, j] * (mine - values[d])
    return mine[:, 0:CZ], total[:, 0:CZ] * diag_ref[x, j]


def twice(x, half):
    lane = iota(x.shape, 1)
    other = pltpu.roll(x, ND, 1)
    return jnp.where(lane < ND, x, other) if half == 0 else jnp.where(lane < ND, other, x)


def ahead_behind(x, step, sign):
    lane = iota(x.shape, 1)
    stride, devices = ((16, 32), (4, 8), (1, 1))[step]
    place = (lane // stride) % 4
    near = pltpu.roll(x, (128 - stride * sign) % 128, 1)
    far = pltpu.roll(x, (3 * stride * sign) % 128, 1)
    far = pltpu.roll(far, (NDEV - devices * sign) % NDEV, 0)
    return jnp.where(place != (3 if sign > 0 else 0), near, far)


def image_kernel(
    pos, p_ref, xa_ref, xb_ref, ya_ref, yb_ref, za_ref, zb_ref, w_ref, diag_ref,
    q_ref, rp_ref, a_ref, b_ref,
    full_ref, plane_ref,
):
    planes = padded_planes(p_ref, Pair(pos, 0, xa_ref, xb_ref))
    wide = Wide(planes, PLACES_2[0], pos, ya_ref, yb_ref, za_ref, zb_ref)
    mask = inside_yz(pos)
    for i in range(PX):
        put(full_ref, i, wide(i) * (mask * inside_x(pos, i - HX)))
    first_scale, _ = recurrence()
    for j in range(ROWS):
        rows = pl.ds(j, 8, stride=ROWS)
        for i in range(1, PX - 1):
            values = around_strided(lambda i, j: strided(full_ref, i, j), i, j)
            mine = strided(full_ref, i, j)
            total = w_ref[0, i, j] * (mine - values[0])
            for d in range(1, 6):
                total = total + w_ref[d, i, j] * (mine - values[d])
            store(rp_ref, i, j, total, HX - 1)
            store(a_ref, i, j, total * first_scale, HX - 1)
            if HX <= i < HX + CX:
                plane_ref[i - HX, rows, :] = total[:, 0:CZ] * diag_ref[i - HX, j]
    chebyshev(HX - 1, w_ref, rp_ref, a_ref, b_ref, (0, 2))
    for x in range(CX):
        q_ref[x] = plane_ref[x, HY : HY + CY]


def smooth_image_kernel(
    w_ref, diag_ref, rp_ref, a_ref, b_ref, p_ref, q_ref, r_ref, v_ref, e_ref,
    c_ref, y_ref, send_ref,
    plane_ref, one_ref, two_ref,
):
    result, _ = chebyshev(HX - 3, w_ref, rp_ref, a_ref, b_ref, (2, DEG - 1), [one_ref, two_ref])
    for x in range(CX):
        for j in range(ROWS):
            rows = pl.ds(j, 8, stride=ROWS)
            mine, image = image_of(result, w_ref, diag_ref, x, j)
            plane_ref[x, rows, :] = mine
            plane_ref[CX + x, rows, :] = image
    parts = [jnp.zeros((CY, CZ), F32) for _ in range(4)]
    energy = jnp.zeros((CY, CZ), F32)
    curve = jnp.zeros((CY, CZ), F32)
    for x in range(CX):
        q = q_ref[x]
        c_ref[x] = plane_ref[x, HY : HY + CY]
        y_ref[x] = plane_ref[CX + x, HY : HY + CY]
        energy = energy + r_ref[x] * p_ref[x]
        curve = curve + q * p_ref[x]
        parts[x // 2] = parts[x // 2] + v_ref[x] * q
    lane = iota((1, 128), 1)
    scalars = jnp.where(lane == 64, total_sum(energy), jnp.where(lane == 65, total_sum(curve), 0.0))
    (row,) = row_sums([parts])
    send = jnp.concatenate(
        [
            jnp.where(lane < ND, row, e_ref[0:1]),
            jnp.where(lane < ND, e_ref[1:2], e_ref[2:3]),
            jnp.where(lane < ND, e_ref[3:4], scalars),
        ],
        axis=1,
    )
    send_ref[...] = jnp.broadcast_to(send, (NDEV, 384))


def first_scalars(sums_ref):
    totals = jnp.sum(sums_ref[:, 256:384], axis=0, keepdims=True)
    energy = totals[0:1, 64:65]
    curve = totals[0:1, 65:66]
    return energy, curve, energy / curve


def amounts_kernel(sums_ref, matrix_ref, p_ref, q_ref, c_ref, y_ref, v_ref, r_ref, send_ref, piece_ref):
    _, _, alpha = first_scalars(sums_ref)
    piece_ref[...] = sums_ref[:, 0:128]
    even = piece_ref[pl.ds(0, 64, stride=2), :]
    odd = pltpu.roll(piece_ref[pl.ds(1, 64, stride=2), :], 64, 1)
    amounts = coarse_rows(matrix_ref, even, odd)
    (field,) = fields([amounts])
    sums = [jnp.zeros((CY, CZ), F32) for _ in range(3)]
    for x in range(CX):
        lifted = v_ref[x] * plane_field(field, x // 2)
        p, q, c = p_ref[x], q_ref[x], c_ref[x]
        residual = r_ref[x] - alpha * q
        smooth = p - alpha * c
        smooth_image = q - alpha * y_ref[x]
        precond = smooth - alpha * lifted
        sums[0] = sums[0] + residual * precond
        sums[1] = sums[1] + precond * q
        sums[2] = sums[2] + smooth_image * (smooth - 2.0 * alpha * lifted)
    lane = iota((1, 128), 1)
    row = jnp.where(lane < ND, amounts, 0.0)
    for n in range(3):
        row = jnp.where(lane == ND + n, total_sum(sums[n]), row)
    send_ref[...] = jnp.broadcast_to(row, (NDEV, 128))


def final_kernel(
    pos, sums_ref, got_ref, p_ref, q_ref, c_ref, y_ref, r_ref, vx_ref, w_ref, diag_ref,
    pressure_ref, residual_ref,
    lift_ref, plane_ref,
):
    energy, curve, alpha = first_scalars(sums_ref)
    got = got_ref[...]
    dup = twice(got, 0)
    half = twice(sums_ref[:, 0:128], 1) * dup
    towards = (twice(sums_ref[:, 128:256], 0), twice(sums_ref[:, 128:256], 1), twice(sums_ref[:, 256:384], 0))
    for step in range(3):
        half = half + 2.0 * towards[step] * ahead_behind(dup, step, 1)
    quad = total_sum(jnp.where(iota((NDEV, 128), 1) < ND, half * dup, 0.0))
    totals = jnp.sum(got, axis=0, keepdims=True)
    energy_next = totals[0:1, 64:65]
    mixed = totals[0:1, 65:66]
    beta = energy_next / energy
    curve_next = totals[0:1, 66:67] + alpha * alpha * quad + 2.0 * beta * mixed + beta * beta * curve
    alpha_next = energy_next / curve_next

    me = (pos[0] * 4 + pos[1]) * 8 + pos[2]
    rows = []
    for shift in (0, -32, 32, -8, 8, -1, 1):
        at = jnp.clip(me + shift, 0, NDEV - 1)
        rows.append(got_ref[pl.ds(at, 1), :])
    mine, xm, xp, ym, yp, zm, zp = fields(rows)
    lanes = iota((PY, CZ), 1)
    zeros = jnp.zeros((HY, CZ), F32)
    for i in range(N_V):
        x = i - H_V
        if x < 0 or x >= CX:
            own = plane_field(xm, 3) if x < 0 else plane_field(xp, 0)
            middle = jnp.concatenate([zeros, own, zeros], axis=0)
            side = jnp.zeros((PY, CZ), F32)
        else:
            s = x // 2
            down = jnp.broadcast_to(ym[4 * s + 3 : 4 * s + 4], (HY, CZ))
            up = jnp.broadcast_to(yp[4 * s : 4 * s + 1], (HY, CZ))
            middle = jnp.concatenate([down, plane_field(mine, s), up], axis=0)
            ahead = jnp.concatenate([zeros, plane_field(zp, s), zeros], axis=0)
            behind = jnp.concatenate([zeros, plane_field(zm, s), zeros], axis=0)
            side = jnp.where(lanes < 8, ahead, jnp.where(lanes >= CZ - 8, behind, 0.0))
        lift_ref[0, i] = vx_ref[0, i] * middle
        lift_ref[1, i] = vx_ref[1, i] * side
    for x in range(CX):
        for j in range(ROWS):
            values = around_strided(lambda i, j: strided(lift_ref, i, j), x + H_V, j)
            mine = strided(lift_ref, x + H_V, j)
            total = w_ref[0, x + HX, j] * (mine - values[0])
            for d in range(1, 6):
                total = total + w_ref[d, x + HX, j] * (mine - values[d])
            plane_ref[x, pl.ds(j, 8, stride=ROWS), :] = total[:, 0:CZ] * diag_ref[x, j]
        lifted_image = plane_ref[x, HY : HY + CY]
        lifted = lift_ref[0, x + H_V, HY : HY + CY]
        p, q = p_ref[x], q_ref[x]
        precond = p - alpha * (c_ref[x] + lifted)
        precond_image = q - alpha * (y_ref[x] + lifted_image)
        direction = precond + beta * p
        image = precond_image + beta * q
        pressure_ref[x] = alpha * p + alpha_next * direction
        residual_ref[x] = (r_ref[x] - alpha * q) - alpha_next * image


VMEM = pl.BlockSpec(memory_space=pltpu.VMEM)
SMEM = pl.BlockSpec(memory_space=pltpu.SMEM)


def call(kernel, outs, scratch=(), smem=False, hbm=0, mib=20, cost=None):
    def run(*args):
        many = isinstance(outs, list)
        specs = [VMEM] * len(args)
        if smem:
            specs[0] = SMEM
        for n in range(int(smem), int(smem) + hbm):
            specs[n] = pl.BlockSpec(memory_space=pltpu.HBM)
        return pl.pallas_call(
            kernel,
            out_shape=[jax.ShapeDtypeStruct(s, F32) for s in outs] if many else jax.ShapeDtypeStruct(outs, F32),
            in_specs=specs,
            out_specs=[VMEM] * len(outs) if many else VMEM,
            scratch_shapes=[pltpu.VMEM(s, F32) if isinstance(s, tuple) else s for s in scratch],
            compiler_params=pltpu.CompilerParams(vmem_limit_bytes=mib * 1024 * 1024),
            cost_estimate=cost,
        )(*args)

    return run


def cost(us):
    return pl.CostEstimate(flops=int(us * 1e6), bytes_accessed=int(us * 3e6), transcendentals=0)


def swap(a, b, axis):
    count = lax.axis_size(axis)
    got_a = lax.ppermute(a, axis, [(i, i ^ 1) for i in range(count)])
    got_b = lax.ppermute(b, axis, [(i, (i - 1 if i % 2 == 0 else i + 1) % count) for i in range(count)])
    return got_a, got_b


def gather(rows):
    return lax.all_to_all(rows, AXES, 0, 0, tiled=True)


def exchange_yz(pos, own):
    places, count = PLACES_2 if len(own) == 3 else PLACES_1
    groups = -(-count // 16)
    ya, yb = call(y_kernel, [(count, HY, CZ)] * 2, smem=True)(pos, *own)
    ya, yb = swap(ya, yb, "gy")
    left, right = call(z_own_kernel, [(groups, CY, CZ)] * 2, smem=True, cost=cost(1))(pos, *own)
    pack = functools.partial(z_kernel, places)
    za, zb = call(pack, [(groups, PY, CZ)] * 2, smem=True)(pos, ya, yb, left, right)
    return (ya, yb, *swap(za, zb, "gz"))


def local(right_side, phase, deflation_weights, coarse_inverse):
    pos = jnp.stack([lax.axis_index(a) for a in AXES]).astype(jnp.int32)
    block = (CX, CY, CZ)
    tall = (2, PX, PY, CZ)
    split = (PX, ROWS, 8, PZ)
    n_x = H_R + H_G + H_V
    labels = jnp.where(phase == 1, 1.0, 0.0).astype(F32)
    xa, xb, send, r, g, v = call(
        start_kernel,
        [(n_x, CY, CZ), (n_x, CY, CZ), (NDEV, 128), block, block, block],
        smem=True,
    )(pos, jnp.concatenate([right_side, labels, deflation_weights], axis=0))
    xa, xb = swap(xa, xb, "gx")
    sums = gather(send)
    xa, xb, sums = lax.optimization_barrier((xa, xb, sums))
    own = (r, g, v, xa, xb)
    halos = exchange_yz(pos, own)
    amounts = call(first_amounts_kernel, (1, 128), cost=cost(1))(sums, coarse_inverse)
    p, xa, xb, v_wide, w, diag = call(
        smooth_kernel,
        [block, (HX, CY, CZ), (HX, CY, CZ), (2, N_V, PY, CZ), (6, *split), (CX, ROWS, 8, CZ)],
        scratch=[tall, (2, N_R, PY, CZ), split, split, split, (CX, PY, CZ)],
        smem=True,
    )(pos, *own, *halos, amounts)
    own = (p, *swap(xa, xb, "gx"))
    quads = call(product_kernel, (4, 128), scratch=[(16, PY, CZ)], cost=cost(1))(v_wide, w, diag)
    halos = exchange_yz(pos, own)
    q, scaled, newest, older = call(
        image_kernel, [block, split, split, split], scratch=[tall, (CX, PY, CZ)], smem=True
    )(pos, *own, *halos, w, diag)
    c, y, send = call(
        smooth_image_kernel, [block, block, (NDEV, 384)], scratch=[(2 * CX, PY, CZ), split, split]
    )(w, diag, scaled, newest, older, p, q, r, v, quads)
    sums = gather(send)
    send = call(amounts_kernel, (NDEV, 128), scratch=[(NDEV, 128)])(sums, coarse_inverse, p, q, c, y, v, r)
    got = gather(send)
    pressure, residual = call(
        final_kernel, [block, block], scratch=[(2, N_V, PY, CZ), (CX, PY, CZ)], smem=True
    )(pos, sums, got, p, q, c, y, r, v_wide, w, diag)
    return (pressure, residual)


def solution(mesh):
    return jax.shard_map(
        local,
        mesh=mesh,
        in_specs=(P(*AXES), P(*AXES), P(*AXES), P(AXES, None)),
        out_specs=(P(*AXES), P(*AXES)),
        check_vma=False,
    )
```
